512 devices in a mesh: expert: 16 (over z), replica: 32 (over y, x, core).
Axes of the slice: x: 4, y: 4, z: 16, core: 2. Of those that a mesh axis runs over, the one named last changes fastest.
Arguments:
- grads: bfloat16 [32, 2048, 2560], P('replica', 'expert'), may hold values from -6 to 6
- routes: int32 [32, 2048, 6], P('replica', 'expert'), may hold values from 0 to 15, all different within a row; in each aligned block of 128 rows (0 to 127, 128 to 255, ..., all dimensions but the last counted through in order) at most 56 rows name the same one
- gates: bfloat16 [32, 2048, 6], P('replica', 'expert'), may hold values from 0.049804688 to 0.5
- hidden: bfloat16 [32, 14336, 768], P('replica', 'expert'), may hold values from -0.375 to 0.375
- down_weight: bfloat16 [768, 16, 2560], P('replica', 'expert'), may hold values from -0.21875 to 0.21875
Outputs:
- d_hidden: bfloat16 [32, 14336, 768], P('replica', 'expert')
- down_grad: float32 [768, 16, 2560], P('replica', 'expert')
The draws below stay inside these ranges and needn't reach their ends.
Inputs may be any that keep to these rules, and one draw needn't show every extreme that they name: `routes`: among the 128 tokens of one device no expert is named more than 56 times, and in every draw some expert is named exactly 56 times by the tokens of some device; a token names 6 different experts.
All inputs are finite; a program needn't handle non-finite values.
Results may differ from the reference program's by a relative error of at most 0.019.
Values may be sent and summed in bfloat16 or wider, within the bound.
No kernel may reach another device: no remote copies, remote signals or barrier semaphores. Data moves between devices by JAX's collectives and lax.ppermute only.
A program may use at most 128 MiB of HBM per device.

```python
import math
import jax
import jax.numpy as jnp
import numpy as np
from jax import lax

D = 2560
F = 768
EXP_DEV = 1
TOK_DEV = 128
EXPERTS = 16
TOP = 6
CAP = 56
TOKENS = 2048
ROWS_DEV = 896
N_EXPERT = 16
N_REPLICA = 32


def spiked(array, key, source, target, parts, factor):
    owner, partner = [(jnp.arange(array.shape[dim]) // (array.shape[dim] // parts)).reshape([-1 if axis == dim else 1 for axis in range(array.ndim)]) for dim in (source, target)]
    chosen = jax.random.permutation(key, parts)[partner]
    strong = (owner == chosen) | (owner == (partner + parts // 2) % parts)
    return jnp.where(strong, factor * array, array)


def block_levels(stream_key, dims, shards, least, top_value):
    factor_of = 1.0
    for position, shards_of in shards:
        draws = jax.random.uniform(jax.random.fold_in(jax.random.fold_in(stream_key, 6), position), (shards_of,), jnp.float32, least / len(shards), top_value / len(shards))
        factor_of = factor_of * jnp.repeat(jnp.exp(draws), dims[position] // shards_of).reshape((-1,) + (1,) * (len(dims) - 1 - position))
    return factor_of


def shared_out(stream_key, own, number, rows, amount, top, most, skew):
    sequence = jax.random.permutation(stream_key, amount)
    crowded, usual = shares(amount, rows * top, most, skew, True), shares(amount, rows * top, most, skew, False)
    places = jnp.arange(amount)

    def named(sizes, rotation):
        used = int((sizes > 0).sum())
        fixed = max(1, used // 4)
        moved = fixed + (places - fixed + rotation * (used - fixed)) % max(1, amount - fixed)
        return jnp.zeros((amount,), jnp.int32).at[sequence[jnp.where(places < fixed, places, moved)]].set(jnp.asarray(sizes, jnp.int32))

    sizes = jnp.where(number % 4 == 0, named(crowded, number // 4), named(usual, number - number // 4 - 1))
    mixed = jax.random.permutation(jax.random.fold_in(own, 3), amount)
    donor, sink = mixed[0:amount // 2 * 2:2], mixed[1:amount // 2 * 2:2]
    room = jnp.minimum(sizes[donor] - 1, most - sizes[sink]) // 2
    room = jnp.where((donor == sequence[0]) | (sink == sequence[0]) | (sizes[sink] == 0), 0, jnp.maximum(room, 0))
    moved = jax.random.randint(jax.random.fold_in(own, 4), (amount // 2,), 0, 1 << 20) % (room + 1)
    sizes = sizes.at[donor].add(-moved).at[sink].add(moved)
    labels = jnp.searchsorted(jnp.cumsum(sizes), jnp.arange(rows * top), side="right").astype(jnp.int32)
    table = labels.reshape(top, rows).T
    table = table[jax.random.permutation(jax.random.fold_in(own, 1), rows)]
    rotation = jax.random.randint(jax.random.fold_in(own, 2), (rows, 1), 0, top)
    return jnp.take_along_axis(table, (jnp.arange(top)[None, :] + rotation) % top, axis=1)


def shares(count, total, reach, slope, full):
    weights = [(1 << 20) // math.isqrt(standing ** slope) + 1 for standing in range(1, count + 1)]
    largest = reach if full else min(reach, max(-(-total // count), total * weights[0] // sum(weights)))
    least = 1 if total - largest >= count - 1 else 0
    given, rest = [largest] + [least] * (count - 1), total - largest - least * (count - 1)
    while rest > 0:
        candidates = [i for i in range(1, count) if given[i] < largest] or [i for i in range(1, count) if given[i] < reach]
        pool, remaining = sum([weights[i] for i in candidates]), rest
        for i in candidates:
            addition = min(reach - given[i], max(1, remaining * weights[i] // pool), rest)
            given[i] = given[i] + addition
            rest = rest - addition
    return np.array(given)


def gaussian(stream_key, extent, deviation, limit, cuts=(), held_as=jnp.bfloat16):
    factor_of = block_levels(stream_key, extent, cuts, -0.22, 0.18) if cuts else 1.0
    entries = jax.random.normal(stream_key, extent, jnp.float32) * deviation * factor_of
    return jnp.minimum(jnp.maximum(entries, -limit), limit).astype(held_as)


def noise_with(key, shape, scale, most, shards, heavy, kind=jnp.bfloat16):
    values = scale * jax.random.normal(key, shape, jnp.float32)
    if shards:
        values = values * block_levels(key, shape, shards, -0.22, 0.18)
    return jnp.clip(spiked(values, jax.random.fold_in(key, 3), *heavy), -most, most).astype(kind)


def setup_inputs(seed: int = 0) -> dict:
    arg_keys = jax.random.split(jax.random.key(seed), 6)
    grads = gaussian(arg_keys[0], (N_REPLICA, TOKENS, D), 1.0, 6.0, ((0, 32), (1, 16)))
    routes_keys = jax.random.split(jax.random.fold_in(arg_keys[1], 1), N_REPLICA * TOKENS // TOK_DEV)
    routes_turns = jax.random.permutation(jax.random.fold_in(arg_keys[1], 3), N_REPLICA * TOKENS // TOK_DEV)
    routes = jax.vmap(lambda own, number: shared_out(jax.random.fold_in(arg_keys[1], 2), own, number, TOK_DEV, EXPERTS, TOP, CAP, 2))(routes_keys, routes_turns).reshape((N_REPLICA, TOKENS, TOP))
    gates = jnp.clip(0.049804688 + 0.4501953 * jax.random.uniform(arg_keys[2], (N_REPLICA, TOKENS, TOP), jnp.float32) ** block_levels(arg_keys[2], (N_REPLICA, TOKENS, TOP), ((0, 32), (1, 16)), -0.2, 0.2), 0.049804688, 0.5).astype(jnp.bfloat16)
    hidden = noise_with(arg_keys[3], (N_REPLICA, N_EXPERT * ROWS_DEV, F), 0.03, 0.375, ((0, 32), (1, 16)), (0, 2, 32, 2.75))
    down_weight = gaussian(arg_keys[4], (F, EXPERTS, D), F ** -0.5, 0.21875, ((0, 32), (1, 16)))
    return {"grads": grads, "routes": routes, "gates": gates, "hidden": hidden, "down_weight": down_weight}


def dispatch(grad_rows, route_rows, gate_rows):
    blocks = route_rows.reshape(N_EXPERT, TOK_DEV * TOP)
    onehot = (blocks[:, :, None] == jnp.arange(EXPERTS, dtype=jnp.int32)[None, None, :]).astype(jnp.int32)
    slot_rank = jnp.sum((jnp.cumsum(onehot, axis=1) - 1) * onehot, axis=2).astype(jnp.int32)
    owner_idx = blocks // EXP_DEV
    local_idx = blocks % EXP_DEV
    source = jnp.arange(N_EXPERT, dtype=jnp.int32)[:, None]
    target = owner_idx * ROWS_DEV + (source * EXP_DEV + local_idx) * CAP + slot_rank
    slot_rows = (grad_rows.astype(jnp.float32)[:, None, :] * gate_rows.astype(jnp.float32)[:, :, None]).astype(jnp.bfloat16)
    slot_rows = slot_rows.reshape(TOKENS * TOP, D)
    dispatched = jnp.zeros((N_EXPERT * ROWS_DEV, D), jnp.bfloat16)
    return dispatched.at[target.reshape(TOKENS * TOP).astype(jnp.int32)].set(slot_rows)


def reference(grads, routes, gates, hidden, down_weight):
    weights_f = down_weight.astype(jnp.float32).reshape(F, N_EXPERT, EXP_DEV, D)

    def one_replica(running, inputs):
        grad_rows, route_rows, gate_rows, saved = inputs
        dispatched = dispatch(grad_rows, route_rows, gate_rows)
        spread = dispatched.astype(jnp.float32).reshape(N_EXPERT, N_EXPERT, EXP_DEV, CAP, D)
        saved_f = saved.astype(jnp.float32).reshape(N_EXPERT, N_EXPERT, EXP_DEV, CAP, F)
        d_rows = jnp.einsum('osjcd,fojd->osjcf', spread, weights_f, precision=lax.Precision.HIGHEST)
        d_rows = d_rows.astype(jnp.bfloat16).reshape(N_EXPERT * ROWS_DEV, F)
        partial_value = jnp.einsum('osjcf,osjcd->fojd', saved_f, spread, precision=lax.Precision.HIGHEST)
        partial_value = lax.optimization_barrier(partial_value.astype(jnp.bfloat16))
        running = running + partial_value.astype(jnp.float32).reshape(F, EXPERTS, D)
        return running, d_rows

    start_sum = jnp.zeros((F, EXPERTS, D), jnp.float32)
    down_grad, d_hidden = lax.scan(one_replica, start_sum, (grads, routes, gates, hidden))
    return d_hidden, down_grad
```

```python
import jax
import jax.numpy as jnp
from jax import lax
from jax.experimental import pallas as pl
from jax.experimental.pallas import tpu as pltpu
from jax.sharding import PartitionSpec as P

BF = jnp.bfloat16
F32 = jnp.float32
LANES = 128
INFO_ROWS = 8


def _info_kernel(routes_ref, gates_ref, info_ref):
    tokens, top = routes_ref.shape
    routes = routes_ref[...]
    gates = gates_ref[...].astype(F32)
    lane = lax.broadcasted_iota(jnp.int32, (tokens, LANES), 1)
    gate = jnp.zeros((tokens, LANES), F32)
    named = jnp.zeros((tokens, LANES), F32)
    for k in range(top):
        hit = routes[:, k : k + 1] == lane
        gate = jnp.where(hit, gates[:, k : k + 1], gate)
        named = jnp.where(hit, 1.0, named)
    row = lax.broadcasted_iota(jnp.int32, (tokens, tokens), 0)
    col = lax.broadcasted_iota(jnp.int32, (tokens, tokens), 1)
    earlier = jnp.where(col < row, 1.0, 0.0).astype(BF)
    rank = jnp.dot(earlier, named.astype(BF), preferred_element_type=F32)
    slot = jnp.where(named > 0.5, rank, -1.0)
    slot_t = slot.T
    gate_t = gate.T
    n = INFO_ROWS
    info_ref[...] = jnp.zeros_like(info_ref)
    info_ref[:, 0:tokens] = slot_t[0:n].astype(BF)
    info_ref[:, tokens : 2 * tokens] = gate_t[0:n].astype(BF)
    info_ref[:, 2 * tokens : 3 * tokens] = slot_t[n : 2 * n].astype(BF)
    info_ref[:, 3 * tokens : 4 * tokens] = gate_t[n : 2 * n].astype(BF)


def _info(routes, gates, width):
    return pl.pallas_call(
        _info_kernel,
        out_shape=jax.ShapeDtypeStruct((INFO_ROWS, width), BF),
        cost_estimate=pl.CostEstimate(flops=1 << 22, bytes_accessed=1 << 16, transcendentals=0),
        name="route_info",
    )(routes, gates)


def _select_kernel(count, tokens, meta_ref, *refs):
    firsts, seconds, out_ref = refs[:count], refs[count : 2 * count], refs[-1]
    capacity = out_ref.shape[1]
    half = firsts[0].shape[1]
    me = meta_ref[0]
    step = pl.program_id(0)
    for i in range(count):

        @pl.when(step == i)
        def _():
            info = seconds[i][tokens : tokens + INFO_ROWS, 0 : 4 * tokens].astype(F32)
            info = jnp.where(me >= INFO_ROWS, info[:, 2 * tokens :], info[:, : 2 * tokens])
            row = lax.broadcasted_iota(jnp.int32, info.shape, 0)
            mine = jnp.sum(jnp.where(row == lax.rem(me, INFO_ROWS), info, 0.0), axis=0, keepdims=True)
            slot = lax.broadcasted_iota(jnp.int32, (capacity, tokens), 0).astype(F32)
            pick = jnp.where(mine[:, :tokens] == slot, mine[:, tokens:], 0.0).astype(BF)
            out_ref[0, :, :half] = jnp.dot(
                pick, firsts[i][0:tokens, :], preferred_element_type=F32
            ).astype(BF)
            out_ref[0, :, half:] = jnp.dot(
                pick, seconds[i][0:tokens, :], preferred_element_type=F32
            ).astype(BF)


def _select(meta, firsts, seconds, rows, shape, name):
    count = len(firsts)
    tokens = firsts[0].shape[0]
    whole = [pl.BlockSpec(a.shape, lambda i, m: (0, 0)) for a in firsts + seconds]
    operands = list(firsts) + list(seconds)
    aliases = {}
    if rows is not None:
        whole.append(pl.BlockSpec(memory_space=pl.ANY))
        operands.append(rows)
        aliases = {1 + 2 * count: 0}

    def kernel(meta_ref, *refs):
        _select_kernel(count, tokens, meta_ref, *refs)

    return pl.pallas_call(
        kernel,
        grid_spec=pltpu.PrefetchScalarGridSpec(
            num_scalar_prefetch=1,
            grid=(count,),
            in_specs=whole,
            out_specs=pl.BlockSpec((1,) + shape[1:], lambda i, m: (m[1 + i], 0, 0)),
        ),
        out_shape=jax.ShapeDtypeStruct(shape, BF),
        input_output_aliases=aliases,
        compiler_params=pltpu.CompilerParams(vmem_limit_bytes=40 << 20),
        cost_estimate=pl.CostEstimate(
            flops=2 * count * shape[1] * tokens * shape[2],
            bytes_accessed=2 * count * (tokens + shape[1]) * shape[2],
            transcendentals=0,
        ),
        name=name,
    )(meta, *operands)


def _term_kernel(saved_ref, rows_ref, out_ref):
    out_ref[...] = jnp.dot(saved_ref[...], rows_ref[...], preferred_element_type=F32).astype(BF)


def _term(saved_t, rows, name):
    units, depth = saved_t.shape
    width = rows.shape[1]
    block = 512 if width % 512 == 0 else LANES
    return pl.pallas_call(
        _term_kernel,
        grid=(width // block,),
        in_specs=[
            pl.BlockSpec((units, depth), lambda j: (0, 0)),
            pl.BlockSpec((depth, block), lambda j: (0, j)),
        ],
        out_specs=pl.BlockSpec((units, block), lambda j: (0, j)),
        out_shape=jax.ShapeDtypeStruct((units, width), BF),
        compiler_params=pltpu.CompilerParams(vmem_limit_bytes=40 << 20),
        cost_estimate=pl.CostEstimate(
            flops=2 * units * depth * width,
            bytes_accessed=2 * (units * depth + depth * width + units * width),
            transcendentals=0,
        ),
        name=name,
    )(saved_t, rows)


def body(grads, routes, gates, hidden, down_weight):
    groups = lax.axis_size("expert")
    replicas = lax.axis_size("replica")
    chips = replicas // 2
    width = grads.shape[2]
    units_dev = down_weight.shape[0]
    rows_dev = hidden.shape[1]
    units = hidden.shape[2]
    capacity = rows_dev // groups
    half = width // 2
    me = lax.axis_index("expert")
    core = lax.rem(lax.axis_index("replica"), 2)

    weights = lax.all_gather(down_weight, "replica", axis=0, tiled=True)

    own_first = grads[0, :, :half]
    own_second = jnp.concatenate(
        [grads[0, :, half:], _info(routes[0], gates[0], half)], axis=0
    )
    up = [(i, (i + 1) % groups) for i in range(groups)]
    down = [(i, (i - 1) % groups) for i in range(groups)]
    far = groups // 2
    got_first, got_second = {0: own_first}, {0: own_second}
    a_up = a_down = own_first
    b_up = b_down = own_second
    for hop in range(1, far + 1):
        a_up = lax.ppermute(a_up, "expert", up)
        if hop < far:
            a_down = lax.ppermute(a_down, "expert", down)
            b_up = lax.ppermute(b_up, "expert", up)
        b_down = lax.ppermute(b_down, "expert", down)
        got_first[-hop], got_second[hop] = a_up, b_down
        if hop < far:
            got_first[hop], got_second[-hop] = a_down, b_up
    got_second[-far] = got_second.pop(far)

    saved_t = hidden[0].T.reshape(chips, 2, units_dev, rows_dev).transpose(1, 0, 2, 3)
    saved_t = saved_t.reshape(2, units // 2, rows_dev)
    saved_mine = lax.dynamic_index_in_dim(saved_t, core, 0, keepdims=False)
    saved_other = lax.dynamic_index_in_dim(saved_t, 1 - core, 0, keepdims=False)

    rows = None
    shape = (groups, capacity, width)
    batches = [
        [0, -1, 1, -2, 2],
        [-3, 3, -4, 4],
        [-5, 5, -6, 6],
        [-7, 7, -8],
    ]
    for number, batch in enumerate(batches):
        source = [lax.rem(me + off + groups, groups) for off in batch]
        meta = jnp.stack([me] + source).astype(jnp.int32)
        rows = _select(
            meta,
            [got_first[off] for off in batch],
            [got_second[off] for off in batch],
            rows,
            shape,
            f"select_{number}",
        )
    rows = rows.reshape(rows_dev, width)

    other = _term(saved_other, rows, "term_other")
    arrived = lax.ppermute(other, "replica", [(i, i ^ 1) for i in range(replicas)])
    mine = _term(saved_mine, rows, "term_mine")
    pair = (mine.astype(F32) + arrived.astype(F32)).astype(BF)
    parts = lax.all_to_all(
        pair.reshape(chips, units_dev, width),
        "replica",
        split_axis=0,
        concat_axis=0,
        tiled=True,
        axis_index_groups=[[2 * q + c for q in range(chips)] for c in range(2)],
    )
    down_grad = jnp.sum(parts.astype(F32), axis=0)[:, None, :]

    d_rows = lax.dot_general(
        rows, weights[:, 0, :], (((1,), (1,)), ((), ())), preferred_element_type=F32
    )
    d_hidden = d_rows.astype(BF)[None]
    return (d_hidden, down_grad)


def solution(mesh):
    placed = (P("replica", "expert", None),) * 5
    return jax.shard_map(
        body,
        mesh=mesh,
        in_specs=placed,
        out_specs=(P("replica", "expert", None), P("replica", "expert", None)),
        check_vma=False,
    )
```

```python
import jax
import jax.numpy as jnp
import numpy as np
from jax import lax
from jax.experimental import pallas as pl
from jax.experimental.pallas import tpu as pltpu
from jax.sharding import PartitionSpec as P

BF = jnp.bfloat16
F32 = jnp.float32
LANES = 128
INFO_ROWS = 8


def _info_kernel(routes_ref, gates_ref, info_ref):
    top, tokens = routes_ref.shape
    experts = 2 * INFO_ROWS
    routes = routes_ref[...]
    gates = gates_ref[...].astype(F32)
    expert = lax.broadcasted_iota(jnp.int32, (experts, tokens), 0)
    gate = jnp.zeros((experts, tokens), F32)
    named = jnp.zeros((experts, tokens), F32)
    for k in range(top):
        hit = routes[k : k + 1, :] == expert
        gate = jnp.where(hit, gates[k : k + 1, :], gate)
        named = jnp.where(hit, 1.0, named)
    row = lax.broadcasted_iota(jnp.int32, (tokens, tokens), 0)
    col = lax.broadcasted_iota(jnp.int32, (tokens, tokens), 1)
    earlier = jnp.where(row < col, 1.0, 0.0).astype(BF)
    rank = jnp.dot(named.astype(BF), earlier, preferred_element_type=F32)
    slot = jnp.where(named > 0.5, rank, -1.0)
    n = INFO_ROWS
    info_ref[...] = jnp.zeros_like(info_ref)
    info_ref[:, 0:tokens] = slot[0:n].astype(BF)
    info_ref[:, tokens : 2 * tokens] = gate[0:n].astype(BF)
    info_ref[:, 2 * tokens : 3 * tokens] = slot[n : 2 * n].astype(BF)
    info_ref[:, 3 * tokens : 4 * tokens] = gate[n : 2 * n].astype(BF)


def _info(routes_t, gates_t, width):
    return pl.pallas_call(
        _info_kernel,
        out_shape=jax.ShapeDtypeStruct((INFO_ROWS, width), BF),
        cost_estimate=pl.CostEstimate(flops=1 << 20, bytes_accessed=1 << 16, transcendentals=0),
        name="route_info",
    )(routes_t, gates_t)


def _split_kernel(units_dev, core_ref, hidden_ref, mine_ref, other_ref):
    block, units = hidden_ref.shape
    turned = hidden_ref[...].astype(F32).T.reshape(units // (2 * units_dev), 2, units_dev, block)
    even = turned[:, 0].reshape(units // 2, block)
    odd = turned[:, 1].reshape(units // 2, block)
    first = core_ref[0] == 0
    mine_ref[...] = jnp.where(first, even, odd).astype(BF)
    other_ref[...] = jnp.where(first, odd, even).astype(BF)


def _split(hidden, core, units_dev):
    rows, units = hidden.shape
    block = LANES

    def kernel(*refs):
        _split_kernel(units_dev, *refs)

    return pl.pallas_call(
        kernel,
        grid_spec=pltpu.PrefetchScalarGridSpec(
            num_scalar_prefetch=1,
            grid=(rows // block,),
            in_specs=[pl.BlockSpec((block, units), lambda i, m: (i, 0))],
            out_specs=[pl.BlockSpec((units // 2, block), lambda i, m: (0, i))] * 2,
        ),
        out_shape=[jax.ShapeDtypeStruct((units // 2, rows), BF)] * 2,
        cost_estimate=pl.CostEstimate(
            flops=rows * units, bytes_accessed=4 * rows * units, transcendentals=0
        ),
        name="split_hidden",
    )(core, hidden)


def _select_kernel(count, tokens, me_ref, _, *refs):
    firsts, seconds, out_ref = refs[:count], refs[count : 2 * count], refs[-1]
    capacity = out_ref.shape[1]
    half = firsts[0].shape[1]
    me = me_ref[0]
    step = pl.program_id(0)
    for i in range(count):

        @pl.when(step == i)
        def _():
            info = seconds[i][tokens : tokens + INFO_ROWS, 0 : 4 * tokens].astype(F32)
            info = jnp.where(me >= INFO_ROWS, info[:, 2 * tokens :], info[:, : 2 * tokens])
            row = lax.broadcasted_iota(jnp.int32, info.shape, 0)
            mine = jnp.sum(jnp.where(row == lax.rem(me, INFO_ROWS), info, 0.0), axis=0, keepdims=True)
            slot = lax.broadcasted_iota(jnp.int32, (capacity, tokens), 0).astype(F32)
            pick = jnp.where(mine[:, :tokens] == slot, mine[:, tokens:], 0.0).astype(BF)
            out_ref[0, :, :half] = jnp.dot(
                pick, firsts[i][0:tokens, :], preferred_element_type=F32
            ).astype(BF)
            out_ref[0, :, half:] = jnp.dot(
                pick, seconds[i][0:tokens, :], preferred_element_type=F32
            ).astype(BF)


def _select(me, offsets, firsts, seconds, rows, shape, name):
    count = len(firsts)
    groups = shape[0]
    steps = np.array([(off + groups) % groups for off in offsets], np.int32)
    tokens = firsts[0].shape[0]
    whole = [pl.BlockSpec(a.shape, lambda i, m, o: (0, 0)) for a in firsts + seconds]
    operands = list(firsts) + list(seconds)
    aliases = {}
    if rows is not None:
        whole.append(pl.BlockSpec(memory_space=pl.ANY))
        operands.append(rows)
        aliases = {2 + 2 * count: 0}

    def kernel(*refs):
        _select_kernel(count, tokens, *refs)

    return pl.pallas_call(
        kernel,
        grid_spec=pltpu.PrefetchScalarGridSpec(
            num_scalar_prefetch=2,
            grid=(count,),
            in_specs=whole,
            out_specs=pl.BlockSpec(
                (1,) + shape[1:], lambda i, m, o: (lax.rem(m[0] + o[i], groups), 0, 0)
            ),
        ),
        out_shape=jax.ShapeDtypeStruct(shape, BF),
        input_output_aliases=aliases,
        compiler_params=pltpu.CompilerParams(vmem_limit_bytes=40 << 20),
        cost_estimate=pl.CostEstimate(
            flops=2 * count * shape[1] * tokens * shape[2],
            bytes_accessed=2 * count * (tokens + shape[1]) * shape[2],
            transcendentals=0,
        ),
        name=name,
    )(me, steps, *operands)


def _term_kernel(saved_ref, rows_ref, out_ref):
    out_ref[...] = jnp.dot(saved_ref[...], rows_ref[...], preferred_element_type=F32).astype(BF)


def _term(saved_t, rows, name):
    units, depth = saved_t.shape
    width = rows.shape[1]
    block = 512 if width % 512 == 0 else LANES
    return pl.pallas_call(
        _term_kernel,
        grid=(width // block,),
        in_specs=[
            pl.BlockSpec((units, depth), lambda j: (0, 0)),
            pl.BlockSpec((depth, block), lambda j: (0, j)),
        ],
        out_specs=pl.BlockSpec((units, block), lambda j: (0, j)),
        out_shape=jax.ShapeDtypeStruct((units, width), BF),
        compiler_params=pltpu.CompilerParams(vmem_limit_bytes=40 << 20),
        cost_estimate=pl.CostEstimate(
            flops=2 * units * depth * width,
            bytes_accessed=2 * (units * depth + depth * width + units * width),
            transcendentals=0,
        ),
        name=name,
    )(saved_t, rows)


def body(grads, routes, gates, hidden, down_weight):
    groups = lax.axis_size("expert")
    replicas = lax.axis_size("replica")
    chips = replicas // 2
    width = grads.shape[2]
    units_dev = down_weight.shape[0]
    rows_dev = hidden.shape[1]
    units = hidden.shape[2]
    capacity = rows_dev // groups
    half = width // 2
    me = lax.axis_index("expert").astype(jnp.int32).reshape(1)
    core = lax.rem(lax.axis_index("replica"), 2)

    weights = lax.all_gather(down_weight, "replica", axis=0, tiled=True)

    own_first = grads[0, :, :half]
    info = _info(routes[0].T, gates[0].T, half)
    own_second = jnp.concatenate([grads[0, :, half:], info], axis=0)
    hidden, own_second = lax.optimization_barrier((hidden, own_second))
    saved_mine, saved_other = _split(hidden[0], core.reshape(1), units_dev)

    up = [(i, (i + 1) % groups) for i in range(groups)]
    down = [(i, (i - 1) % groups) for i in range(groups)]
    far = groups // 2
    got_first, got_second = {0: own_first}, {0: own_second}
    a_up = a_down = own_first
    b_up = b_down = own_second
    for hop in range(1, far + 1):
        if hop == 2:
            a_up, saved_mine, saved_other = lax.optimization_barrier(
                (a_up, saved_mine, saved_other)
            )
        if hop == far:
            me, a_up, a_down, b_up, b_down = lax.optimization_barrier(
                (me, a_up, a_down, b_up, b_down)
            )
        a_up = lax.ppermute(a_up, "expert", up)
        if hop < far:
            a_down = lax.ppermute(a_down, "expert", down)
            b_up = lax.ppermute(b_up, "expert", up)
        b_down = lax.ppermute(b_down, "expert", down)
        got_first[-hop], got_second[hop] = a_up, b_down
        if hop < far:
            got_first[hop], got_second[-hop] = a_down, b_up
    got_second[-far] = got_second.pop(far)

    rows = None
    shape = (groups, capacity, width)
    batches = [
        [0, -1, 1, -2, 2],
        [-3, 3, -4, 4],
        [-5, 5, -6, 6, -7, 7],
        [-8],
    ]
    for number, batch in enumerate(batches):
        rows = _select(
            me,
            batch,
            [got_first[off] for off in batch],
            [got_second[off] for off in batch],
            rows,
            shape,
            f"select_{number}",
        )
    rows = rows.reshape(rows_dev, width)

    other = _term(saved_other, rows, "term_other")
    arrived = lax.ppermute(other, "replica", [(i, i ^ 1) for i in range(replicas)])
    mine = _term(saved_mine, rows, "term_mine")
    pair = (mine.astype(F32) + arrived.astype(F32)).astype(BF)
    pair, rows, weights = lax.optimization_barrier((pair, rows, weights))
    parts = lax.all_to_all(
        pair.reshape(chips, units_dev, width),
        "replica",
        split_axis=0,
        concat_axis=0,
        tiled=True,
        axis_index_groups=[[2 * q + c for q in range(chips)] for c in range(2)],
    )
    d_rows = lax.dot_general(
        rows, weights[:, 0, :], (((1,), (1,)), ((), ())), preferred_element_type=F32
    )
    d_hidden = d_rows.astype(BF)[None]
    parts, d_hidden = lax.optimization_barrier((parts, d_hidden))
    down_grad = jnp.sum(parts.astype(F32), axis=0)[:, None, :]
    return (d_hidden, down_grad)


def solution(mesh):
    placed = (P("replica", "expert", None),) * 5
    return jax.shard_map(
        body,
        mesh=mesh,
        in_specs=placed,
        out_specs=(P("replica", "expert", None), P("replica", "expert", None)),
        check_vma=False,
    )
```

```python
import jax
import jax.numpy as jnp
from jax import lax
from jax.experimental import pallas as pl
from jax.experimental.pallas import tpu as pltpu
from jax.sharding import PartitionSpec as P

BF = jnp.bfloat16
F32 = jnp.float32
LANES = 128
INFO_ROWS = 8
VMEM = 16 << 20


def _pack_kernel(grads_ref, routes_ref, gates_ref, first_ref, second_ref):
    top, _, tokens = routes_ref.shape
    half = first_ref.shape[1]
    experts = 2 * INFO_ROWS
    first_ref[...] = grads_ref[:, 0:half]
    second_ref[0:tokens, :] = grads_ref[:, half:]
    gates = gates_ref[...].astype(F32)
    expert = lax.broadcasted_iota(jnp.int32, (experts, tokens), 0)
    gate = jnp.zeros((experts, tokens), F32)
    named = jnp.zeros((experts, tokens), F32)
    for k in range(top):
        hit = routes_ref[k] == expert
        gate = jnp.where(hit, gates[k : k + 1, :], gate)
        named = jnp.where(hit, 1.0, named)
    row = lax.broadcasted_iota(jnp.int32, (tokens, tokens), 0)
    col = lax.broadcasted_iota(jnp.int32, (tokens, tokens), 1)
    earlier = jnp.where(row < col, 1.0, 0.0).astype(BF)
    rank = jnp.dot(named.astype(BF), earlier, preferred_element_type=F32)
    slot = jnp.where(named > 0.5, rank, -1.0)
    n = INFO_ROWS
    parts = [slot[0:n], gate[0:n], slot[n : 2 * n], gate[n : 2 * n]]
    parts.append(jnp.zeros((n, half - 4 * tokens), F32))
    second_ref[tokens : tokens + n, :] = jnp.concatenate(parts, axis=1).astype(BF)


def _pack(grads, routes_t, gates_t):
    tokens, width = grads.shape
    half = width // 2
    return pl.pallas_call(
        _pack_kernel,
        out_shape=[
            jax.ShapeDtypeStruct((tokens, half), BF),
            jax.ShapeDtypeStruct((tokens + INFO_ROWS, half), BF),
        ],
        compiler_params=pltpu.CompilerParams(vmem_limit_bytes=VMEM),
        cost_estimate=pl.CostEstimate(
            flops=1 << 20, bytes_accessed=4 * tokens * width, transcendentals=0
        ),
        name="pack_tokens",
    )(grads, routes_t, gates_t)


def _split_kernel(units_dev, core_ref, hidden_ref, mine_ref, other_ref):
    units = hidden_ref.shape[1]
    half = units // 2
    row = lax.broadcasted_iota(jnp.int32, (half, units), 0)
    col = lax.broadcasted_iota(jnp.int32, (half, units), 1)
    even = row + units_dev * (row // units_dev)
    for flip, out_ref in ((0, mine_ref), (1, other_ref)):
        core = lax.rem(core_ref[0] + flip, 2)
        pick = jnp.where(col == even + core * units_dev, 1.0, 0.0).astype(BF)
        out_ref[...] = lax.dot_general(
            pick, hidden_ref[...], (((1,), (1,)), ((), ())), preferred_element_type=F32
        ).astype(BF)


def _split(hidden, core, units_dev):
    rows, units = hidden.shape

    def kernel(*refs):
        _split_kernel(units_dev, *refs)

    return pl.pallas_call(
        kernel,
        grid_spec=pltpu.PrefetchScalarGridSpec(
            num_scalar_prefetch=1,
            grid=(1,),
            in_specs=[pl.BlockSpec((rows, units), lambda i, m: (0, 0))],
            out_specs=[pl.BlockSpec((units // 2, rows), lambda i, m: (0, 0))] * 2,
        ),
        out_shape=[jax.ShapeDtypeStruct((units // 2, rows), BF)] * 2,
        compiler_params=pltpu.CompilerParams(vmem_limit_bytes=VMEM),
        cost_estimate=pl.CostEstimate(
            flops=2 * rows * units * units, bytes_accessed=4 * rows * units, transcendentals=0
        ),
        name="split_hidden",
    )(core, hidden)


def _select_kernel(count, tokens, me_ref, *refs):
    firsts, seconds, out_ref = refs[:count], refs[count : 2 * count], refs[-1]
    capacity = out_ref.shape[1]
    half = firsts[0].shape[1]
    me = me_ref[0]
    step = pl.program_id(0)
    for i in range(count):

        @pl.when(step == i)
        def _():
            info = seconds[i][tokens : tokens + INFO_ROWS, 0 : 4 * tokens].astype(F32)
            info = jnp.where(me >= INFO_ROWS, info[:, 2 * tokens :], info[:, : 2 * tokens])
            row = lax.broadcasted_iota(jnp.int32, info.shape, 0)
            mine = jnp.sum(jnp.where(row == lax.rem(me, INFO_ROWS), info, 0.0), axis=0, keepdims=True)
            slot = lax.broadcasted_iota(jnp.int32, (capacity, tokens), 0).astype(F32)
            pick = jnp.where(mine[:, :tokens] == slot, mine[:, tokens:], 0.0).astype(BF)
            out_ref[0, :, :half] = jnp.dot(
                pick, firsts[i][0:tokens, :], preferred_element_type=F32
            ).astype(BF)
            out_ref[0, :, half:] = jnp.dot(
                pick, seconds[i][0:tokens, :], preferred_element_type=F32
            ).astype(BF)


def _select(me, offsets, firsts, seconds, rows, shape, name):
    count = len(firsts)
    groups = shape[0]
    steps = [(off + groups) % groups for off in offsets]

    def place(i, m):
        step = steps[0]
        for k in range(1, count):
            step = jnp.where(i == k, steps[k], step)
        return (lax.rem(m[0] + step, groups), 0, 0)

    tokens = firsts[0].shape[0]
    whole = [pl.BlockSpec(a.shape, lambda i, m: (0, 0)) for a in firsts + seconds]
    operands = list(firsts) + list(seconds)
    aliases = {}
    if rows is not None:
        whole.append(pl.BlockSpec(memory_space=pltpu.HBM))
        operands.append(rows)
        aliases = {1 + 2 * count: 0}

    def kernel(*refs):
        _select_kernel(count, tokens, *refs)

    return pl.pallas_call(
        kernel,
        grid_spec=pltpu.PrefetchScalarGridSpec(
            num_scalar_prefetch=1,
            grid=(count,),
            in_specs=whole,
            out_specs=pl.BlockSpec((1,) + shape[1:], place),
        ),
        out_shape=pltpu.HBM(shape, BF),
        input_output_aliases=aliases,
        compiler_params=pltpu.CompilerParams(vmem_limit_bytes=VMEM),
        cost_estimate=pl.CostEstimate(
            flops=2 * count * shape[1] * tokens * shape[2],
            bytes_accessed=2 * count * (tokens + shape[1]) * shape[2],
            transcendentals=0,
        ),
        name=name,
    )(me, *operands)


def _term_kernel(saved_ref, rows_ref, out_ref):
    out_ref[...] = jnp.dot(saved_ref[...], rows_ref[...], preferred_element_type=F32).astype(BF)


def _term(saved_t, rows, name):
    units, depth = saved_t.shape
    width = rows.shape[1]
    block = 512 if width % 512 == 0 else LANES
    return pl.pallas_call(
        _term_kernel,
        grid=(width // block,),
        in_specs=[
            pl.BlockSpec((units, depth), lambda j: (0, 0)),
            pl.BlockSpec((depth, block), lambda j: (0, j)),
        ],
        out_specs=pl.BlockSpec((units, block), lambda j: (0, j)),
        out_shape=jax.ShapeDtypeStruct((units, width), BF),
        compiler_params=pltpu.CompilerParams(vmem_limit_bytes=VMEM),
        cost_estimate=pl.CostEstimate(
            flops=2 * units * depth * width,
            bytes_accessed=2 * (units * depth + depth * width + units * width),
            transcendentals=0,
        ),
        name=name,
    )(saved_t, rows)


def body(grads, routes, gates, hidden, down_weight):
    groups = lax.axis_size("expert")
    replicas = lax.axis_size("replica")
    chips = replicas // 2
    width = grads.shape[2]
    units_dev = down_weight.shape[0]
    rows_dev = hidden.shape[1]
    units = hidden.shape[2]
    capacity = rows_dev // groups
    half = width // 2
    me = lax.axis_index("expert").astype(jnp.int32).reshape(1)
    core = lax.rem(lax.axis_index("replica"), 2)

    weights = lax.all_gather(down_weight, "replica", axis=0, tiled=True)

    own_first, own_second = _pack(grads[0], routes.transpose(2, 0, 1), gates[0].T)

    up = [(i, (i + 1) % groups) for i in range(groups)]
    down = [(i, (i - 1) % groups) for i in range(groups)]
    far = groups // 2
    got_first, got_second = {0: own_first}, {0: own_second}
    a_up = a_down = own_first
    b_up = b_down = own_second
    rows = None
    shape = (groups, capacity, width)

    def pick(rows, batch, name):
        firsts = [got_first[off] for off in batch]
        seconds = [got_second[off] for off in batch]
        return _select(me, batch, firsts, seconds, rows, shape, name)

    for hop in range(1, far + 1):
        if 3 <= hop < far:
            a_up, rows = lax.optimization_barrier((a_up, rows))
        if hop == far:
            me, hidden, a_up = lax.optimization_barrier((me, hidden, a_up))
        a_up = lax.ppermute(a_up, "expert", up)
        if hop < far:
            a_down = lax.ppermute(a_down, "expert", down)
            b_up = lax.ppermute(b_up, "expert", up)
        b_down = lax.ppermute(b_down, "expert", down)
        got_first[-hop], got_second[hop] = a_up, b_down
        if hop < far:
            got_first[hop], got_second[-hop] = a_down, b_up
        if hop == 2:
            rows = pick(rows, [0, -1, 1], "select_1")
        elif 3 <= hop < far - 1:
            rows = pick(rows, [1 - hop, hop - 1], f"select_{hop - 1}")
    got_second[-far] = got_second.pop(far)

    rows = pick(rows, [2 - far, far - 2, 1 - far, far - 1], "select_near_last")
    saved_mine, saved_other = _split(hidden[0], core.reshape(1), units_dev)
    rows = pick(rows, [-far], "select_last")
    rows = rows.reshape(rows_dev, width)

    other = _term(saved_other, rows, "term_other")
    arrived = lax.ppermute(other, "replica", [(i, i ^ 1) for i in range(replicas)])
    mine = _term(saved_mine, rows, "term_mine")
    pair = (mine.astype(F32) + arrived.astype(F32)).astype(BF)
    pair, rows, weights = lax.optimization_barrier((pair, rows, weights))
    parts = lax.all_to_all(
        pair.reshape(chips, units_dev, width),
        "replica",
        split_axis=0,
        concat_axis=0,
        tiled=True,
        axis_index_groups=[[2 * q + c for q in range(chips)] for c in range(2)],
    )
    d_rows = lax.dot_general(
        rows, weights[:, 0, :], (((1,), (1,)), ((), ())), preferred_element_type=F32
    )
    d_hidden = d_rows.astype(BF)[None]
    parts, d_hidden = lax.optimization_barrier((parts, d_hidden))
    down_grad = jnp.sum(parts.astype(F32), axis=0)[:, None, :]
    return (d_hidden, down_grad)


def solution(mesh):
    placed = (P("replica", "expert", None),) * 5
    return jax.shard_map(
        body,
        mesh=mesh,
        in_specs=placed,
        out_specs=(P("replica", "expert", None), P("replica", "expert", None)),
        check_vma=False,
    )
```

```python
import jax
import jax.numpy as jnp
from jax import lax
from jax.experimental import pallas as pl
from jax.experimental.pallas import tpu as pltpu
from jax.sharding import PartitionSpec as P

BF = jnp.bfloat16
F32 = jnp.float32
LANES = 128
INFO_ROWS = 8
VMEM = 16 << 20


def _pack_kernel(grads_ref, routes_ref, gates_ref, first_ref, second_ref):
    top, _, tokens = routes_ref.shape
    half = first_ref.shape[1]
    experts = 2 * INFO_ROWS
    first_ref[...] = grads_ref[:, 0:half]
    second_ref[0:tokens, :] = grads_ref[:, half:]
    gates = gates_ref[...].astype(F32)
    expert = lax.broadcasted_iota(jnp.int32, (experts, tokens), 0)
    gate = jnp.zeros((experts, tokens), F32)
    named = jnp.zeros((experts, tokens), F32)
    for k in range(top):
        hit = routes_ref[k] == expert
        gate = jnp.where(hit, gates[k : k + 1, :], gate)
        named = jnp.where(hit, 1.0, named)
    row = lax.broadcasted_iota(jnp.int32, (tokens, tokens), 0)
    col = lax.broadcasted_iota(jnp.int32, (tokens, tokens), 1)
    earlier = jnp.where(row < col, 1.0, 0.0).astype(BF)
    rank = jnp.dot(named.astype(BF), earlier, preferred_element_type=F32)
    slot = jnp.where(named > 0.5, rank, -1.0)
    n = INFO_ROWS
    parts = [slot[0:n], gate[0:n], slot[n : 2 * n], gate[n : 2 * n]]
    parts.append(jnp.zeros((n, half - 4 * tokens), F32))
    second_ref[tokens : tokens + n, :] = jnp.concatenate(parts, axis=1).astype(BF)


def _pack(grads, routes_t, gates_t):
    tokens, width = grads.shape
    half = width // 2
    return pl.pallas_call(
        _pack_kernel,
        out_shape=[
            jax.ShapeDtypeStruct((tokens, half), BF),
            jax.ShapeDtypeStruct((tokens + INFO_ROWS, half), BF),
        ],
        compiler_params=pltpu.CompilerParams(vmem_limit_bytes=VMEM),
        cost_estimate=pl.CostEstimate(
            flops=1 << 20, bytes_accessed=4 * tokens * width, transcendentals=0
        ),
        name="pack_tokens",
    )(grads, routes_t, gates_t)


def _split_kernel(units_dev, core_ref, hidden_ref, mine_ref, other_ref):
    units = hidden_ref.shape[1]
    half = units // 2
    row = lax.broadcasted_iota(jnp.int32, (half, units), 0)
    col = lax.broadcasted_iota(jnp.int32, (half, units), 1)
    even = row + units_dev * (row // units_dev)
    for flip, out_ref in ((0, mine_ref), (1, other_ref)):
        core = lax.rem(core_ref[0] + flip, 2)
        pick = jnp.where(col == even + core * units_dev, 1.0, 0.0).astype(BF)
        out_ref[...] = lax.dot_general(
            pick, hidden_ref[...], (((1,), (1,)), ((), ())), preferred_element_type=F32
        ).astype(BF)


def _split(hidden, core, units_dev):
    rows, units = hidden.shape

    def kernel(*refs):
        _split_kernel(units_dev, *refs)

    return pl.pallas_call(
        kernel,
        in_specs=[
            pl.BlockSpec(memory_space=pltpu.SMEM),
            pl.BlockSpec(memory_space=pltpu.VMEM),
        ],
        out_specs=[pl.BlockSpec(memory_space=pltpu.VMEM)] * 2,
        out_shape=[jax.ShapeDtypeStruct((units // 2, rows), BF)] * 2,
        compiler_params=pltpu.CompilerParams(vmem_limit_bytes=VMEM),
        cost_estimate=pl.CostEstimate(
            flops=2 * rows * units * units, bytes_accessed=4 * rows * units, transcendentals=0
        ),
        name="split_hidden",
    )(core, hidden)


def _picker(expert, second_ref, capacity):
    tokens = second_ref.shape[0] - INFO_ROWS
    info = second_ref[tokens : tokens + INFO_ROWS, 0 : 4 * tokens].astype(F32)
    info = jnp.where(expert >= INFO_ROWS, info[:, 2 * tokens :], info[:, : 2 * tokens])
    row = lax.broadcasted_iota(jnp.int32, info.shape, 0)
    mine = jnp.sum(jnp.where(row == lax.rem(expert, INFO_ROWS), info, 0.0), axis=0, keepdims=True)
    slot = lax.broadcasted_iota(jnp.int32, (capacity, tokens), 0).astype(F32)
    return jnp.where(mine[:, :tokens] == slot, mine[:, tokens:], 0.0).astype(BF)


def _select(me, offsets, firsts, seconds, rows, shape, name):
    count = len(offsets)
    groups, capacity, width = shape
    half = width // 2
    tokens = firsts[0].shape[0]

    def kernel(me_ref, *refs):
        out_ref = refs[-1]
        for i, off in enumerate(offsets):
            first_ref, second_ref = refs[i], refs[count + i]
            pick = _picker(me_ref[0], second_ref, capacity)
            place = lax.rem(me_ref[0] + (off + groups) % groups, groups)
            out_ref[place, :, :half] = jnp.dot(
                pick, first_ref[...], preferred_element_type=F32
            ).astype(BF)
            out_ref[place, :, half:] = jnp.dot(
                pick, second_ref[0:tokens, :], preferred_element_type=F32
            ).astype(BF)

    operands = list(firsts) + list(seconds) + ([] if rows is None else [rows])
    return pl.pallas_call(
        kernel,
        in_specs=[pl.BlockSpec(memory_space=pltpu.SMEM)]
        + [pl.BlockSpec(memory_space=pltpu.VMEM)] * len(operands),
        out_specs=pl.BlockSpec(memory_space=pltpu.VMEM),
        out_shape=jax.ShapeDtypeStruct(shape, BF),
        input_output_aliases={} if rows is None else {len(operands): 0},
        compiler_params=pltpu.CompilerParams(vmem_limit_bytes=VMEM),
        cost_estimate=pl.CostEstimate(
            flops=2 * count * capacity * tokens * width,
            bytes_accessed=2 * count * (tokens + capacity) * width,
            transcendentals=0,
        ),
        name=name,
    )(me, *operands)


def _forward(me, step, block, info_block, rows, name):
    tokens = info_block.shape[0] - INFO_ROWS
    groups, capacity, _ = rows.shape
    width = block.shape[1]

    def kernel(me_ref, block_ref, info_ref, _, out_ref, __):
        expert = lax.rem(me_ref[0] + (step + groups) % groups, groups)
        pick = _picker(expert, info_ref, capacity)
        out_ref[...] = jnp.dot(
            pick, block_ref[0:tokens, :], preferred_element_type=F32
        ).astype(BF)

    return pl.pallas_call(
        kernel,
        in_specs=[pl.BlockSpec(memory_space=pltpu.SMEM)]
        + [pl.BlockSpec(memory_space=pltpu.VMEM)] * 3,
        out_specs=[pl.BlockSpec(memory_space=pltpu.VMEM)] * 2,
        out_shape=[
            jax.ShapeDtypeStruct((capacity, width), BF),
            jax.ShapeDtypeStruct(rows.shape, BF),
        ],
        input_output_aliases={3: 1},
        compiler_params=pltpu.CompilerParams(vmem_limit_bytes=VMEM),
        cost_estimate=pl.CostEstimate(
            flops=2 * capacity * tokens * width,
            bytes_accessed=2 * (tokens + capacity) * width,
            transcendentals=0,
        ),
        name=name,
    )(me, block, info_block, rows)


def _place(me, off, first, second, rows):
    groups, capacity, width = rows.shape
    half = width // 2

    def kernel(me_ref, first_ref, second_ref, _, out_ref):
        place = lax.rem(me_ref[0] + (off + groups) % groups, groups)
        out_ref[place, :, :half] = first_ref[...]
        out_ref[place, :, half:] = second_ref[...]

    return pl.pallas_call(
        kernel,
        in_specs=[pl.BlockSpec(memory_space=pltpu.SMEM)]
        + [pl.BlockSpec(memory_space=pltpu.VMEM)] * 3,
        out_specs=pl.BlockSpec(memory_space=pltpu.VMEM),
        out_shape=jax.ShapeDtypeStruct(rows.shape, BF),
        input_output_aliases={3: 0},
        compiler_params=pltpu.CompilerParams(vmem_limit_bytes=VMEM),
        cost_estimate=pl.CostEstimate(
            flops=0, bytes_accessed=4 * capacity * width, transcendentals=0
        ),
        name="place_last",
    )(me, first, second, rows)


def _term_kernel(saved_ref, rows_ref, out_ref):
    out_ref[...] = jnp.dot(saved_ref[...], rows_ref[...], preferred_element_type=F32).astype(BF)


def _term(saved_t, rows, name):
    units, depth = saved_t.shape
    width = rows.shape[1]
    block = 512 if width % 512 == 0 else LANES
    return pl.pallas_call(
        _term_kernel,
        grid=(width // block,),
        in_specs=[
            pl.BlockSpec((units, depth), lambda j: (0, 0)),
            pl.BlockSpec((depth, block), lambda j: (0, j)),
        ],
        out_specs=pl.BlockSpec((units, block), lambda j: (0, j)),
        out_shape=jax.ShapeDtypeStruct((units, width), BF),
        compiler_params=pltpu.CompilerParams(vmem_limit_bytes=VMEM),
        cost_estimate=pl.CostEstimate(
            flops=2 * units * depth * width,
            bytes_accessed=2 * (units * depth + depth * width + units * width),
            transcendentals=0,
        ),
        name=name,
    )(saved_t, rows)


def body(grads, routes, gates, hidden, down_weight):
    groups = lax.axis_size("expert")
    replicas = lax.axis_size("replica")
    chips = replicas // 2
    width = grads.shape[2]
    units_dev = down_weight.shape[0]
    rows_dev = hidden.shape[1]
    units = hidden.shape[2]
    capacity = rows_dev // groups
    half = width // 2
    me = lax.axis_index("expert").astype(jnp.int32).reshape(1)
    core = lax.rem(lax.axis_index("replica"), 2)

    weights = lax.all_gather(down_weight, "replica", axis=0, tiled=True)

    own_first, own_second = _pack(grads[0], routes.transpose(2, 0, 1), gates[0].T)

    up = [(i, (i + 1) % groups) for i in range(groups)]
    down = [(i, (i - 1) % groups) for i in range(groups)]
    far = groups // 2
    got_first, got_second = {0: own_first}, {0: own_second}
    a_up = a_down = own_first
    b_up = b_down = own_second
    rows = None
    shape = (groups, capacity, width)

    def pick(rows, batch, name):
        firsts = [got_first[off] for off in batch]
        seconds = [got_second[off] for off in batch]
        return _select(me, batch, firsts, seconds, rows, shape, name)

    saved_mine, saved_other = _split(hidden[0], core.reshape(1), units_dev)
    for hop in range(1, far):
        if hop == 2:
            b_up, saved_mine, saved_other = lax.optimization_barrier(
                (b_up, saved_mine, saved_other)
            )
        if hop >= 3:
            a_up, rows = lax.optimization_barrier((a_up, rows))
        a_up = lax.ppermute(a_up, "expert", up)
        a_down = lax.ppermute(a_down, "expert", down)
        b_up = lax.ppermute(b_up, "expert", up)
        b_down = lax.ppermute(b_down, "expert", down)
        got_first[-hop], got_second[hop] = a_up, b_down
        got_first[hop], got_second[-hop] = a_down, b_up
        if hop == 2:
            rows = pick(rows, [0, -1, 1], "select_1")
        elif hop >= 3:
            rows = pick(rows, [1 - hop, hop - 1], f"select_{hop - 1}")

    last_first, rows = _forward(me, 1, a_up, b_up, rows, "forward_up")
    last_first = lax.ppermute(last_first, "expert", up)
    last_second, rows = _forward(me, -1, b_down, b_down, rows, "forward_down")
    last_second = lax.ppermute(last_second, "expert", down)
    rows = pick(rows, [1 - far, far - 1], f"select_{far - 1}")
    rows = _place(me, far, last_first, last_second, rows)
    rows = rows.reshape(rows_dev, width)

    other = _term(saved_other, rows, "term_other")
    arrived = lax.ppermute(other, "replica", [(i, i ^ 1) for i in range(replicas)])
    mine = _term(saved_mine, rows, "term_mine")
    pair = (mine.astype(F32) + arrived.astype(F32)).astype(BF)
    pair, rows, weights = lax.optimization_barrier((pair, rows, weights))
    parts = lax.all_to_all(
        pair.reshape(chips, units_dev, width),
        "replica",
        split_axis=0,
        concat_axis=0,
        tiled=True,
        axis_index_groups=[[2 * q + c for q in range(chips)] for c in range(2)],
    )
    d_rows = lax.dot_general(
        rows, weights[:, 0, :], (((1,), (1,)), ((), ())), preferred_element_type=F32
    )
    d_hidden = d_rows.astype(BF)[None]
    parts, d_hidden = lax.optimization_barrier((parts, d_hidden))
    down_grad = jnp.sum(parts.astype(F32), axis=0)[:, None, :]
    return (d_hidden, down_grad)


def solution(mesh):
    placed = (P("replica", "expert", None),) * 5
    return jax.shard_map(
        body,
        mesh=mesh,
        in_specs=placed,
        out_specs=(P("replica", "expert", None), P("replica", "expert", None)),
        check_vma=False,
    )
```

```python
import jax
import jax.numpy as jnp
from jax import lax
from jax.experimental import pallas as pl
from jax.experimental.pallas import tpu as pltpu
from jax.sharding import PartitionSpec as P

BF = jnp.bfloat16
F32 = jnp.float32
LANES = 128
INFO_ROWS = 8
VMEM = 16 << 20


def _pack_kernel(grads_ref, routes_ref, gates_ref, first_ref, second_ref):
    top, _, tokens = routes_ref.shape
    half = first_ref.shape[1]
    experts = 2 * INFO_ROWS
    first_ref[...] = grads_ref[:, 0:half]
    second_ref[0:tokens, :] = grads_ref[:, half:]
    gates = gates_ref[...].astype(F32)
    expert = lax.broadcasted_iota(jnp.int32, (experts, tokens), 0)
    gate = jnp.zeros((experts, tokens), F32)
    named = jnp.zeros((experts, tokens), F32)
    for k in range(top):
        hit = routes_ref[k] == expert
        gate = jnp.where(hit, gates[k : k + 1, :], gate)
        named = jnp.where(hit, 1.0, named)
    row = lax.broadcasted_iota(jnp.int32, (tokens, tokens), 0)
    col = lax.broadcasted_iota(jnp.int32, (tokens, tokens), 1)
    earlier = jnp.where(row < col, 1.0, 0.0).astype(BF)
    rank = jnp.dot(named.astype(BF), earlier, preferred_element_type=F32)
    slot = jnp.where(named > 0.5, rank, -1.0)
    n = INFO_ROWS
    parts = [slot[0:n], gate[0:n], slot[n : 2 * n], gate[n : 2 * n]]
    parts.append(jnp.zeros((n, half - 4 * tokens), F32))
    second_ref[tokens : tokens + n, :] = jnp.concatenate(parts, axis=1).astype(BF)


def _pack(grads, routes_t, gates_t):
    tokens, width = grads.shape
    half = width // 2
    return pl.pallas_call(
        _pack_kernel,
        out_shape=[
            jax.ShapeDtypeStruct((tokens, half), BF),
            jax.ShapeDtypeStruct((tokens + INFO_ROWS, half), BF),
        ],
        compiler_params=pltpu.CompilerParams(vmem_limit_bytes=VMEM),
        cost_estimate=pl.CostEstimate(
            flops=1 << 20, bytes_accessed=4 * tokens * width, transcendentals=0
        ),
        name="pack_tokens",
    )(grads, routes_t, gates_t)


def _split_kernel(units_dev, core_ref, hidden_ref, mine_ref, other_ref):
    units = hidden_ref.shape[1]
    half = units // 2
    row = lax.broadcasted_iota(jnp.int32, (half, units), 0)
    col = lax.broadcasted_iota(jnp.int32, (half, units), 1)
    even = row + units_dev * (row // units_dev)
    for flip, out_ref in ((0, mine_ref), (1, other_ref)):
        core = lax.rem(core_ref[0] + flip, 2)
        pick = jnp.where(col == even + core * units_dev, 1.0, 0.0).astype(BF)
        out_ref[...] = lax.dot_general(
            pick, hidden_ref[...], (((1,), (1,)), ((), ())), preferred_element_type=F32
        ).astype(BF)


def _split(hidden, core, units_dev):
    rows, units = hidden.shape

    def kernel(*refs):
        _split_kernel(units_dev, *refs)

    return pl.pallas_call(
        kernel,
        in_specs=[
            pl.BlockSpec(memory_space=pltpu.SMEM),
            pl.BlockSpec(memory_space=pltpu.VMEM),
        ],
        out_specs=[pl.BlockSpec(memory_space=pltpu.VMEM)] * 2,
        out_shape=[jax.ShapeDtypeStruct((units // 2, rows), BF)] * 2,
        compiler_params=pltpu.CompilerParams(vmem_limit_bytes=VMEM),
        cost_estimate=pl.CostEstimate(
            flops=2 * rows * units * units, bytes_accessed=4 * rows * units, transcendentals=0
        ),
        name="split_hidden",
    )(core, hidden)


def _picker(expert, second_ref, capacity):
    tokens = second_ref.shape[0] - INFO_ROWS
    info = second_ref[tokens : tokens + INFO_ROWS, 0 : 4 * tokens].astype(F32)
    info = jnp.where(expert >= INFO_ROWS, info[:, 2 * tokens :], info[:, : 2 * tokens])
    row = lax.broadcasted_iota(jnp.int32, info.shape, 0)
    mine = jnp.sum(jnp.where(row == lax.rem(expert, INFO_ROWS), info, 0.0), axis=0, keepdims=True)
    slot = lax.broadcasted_iota(jnp.int32, (capacity, tokens), 0).astype(F32)
    return jnp.where(mine[:, :tokens] == slot, mine[:, tokens:], 0.0).astype(BF)


def _select(me, offsets, firsts, seconds, rows, shape, name, after=()):
    count = len(offsets)
    groups, capacity, width = shape
    half = width // 2
    tokens = firsts[0].shape[0]

    def kernel(me_ref, *refs):
        out_ref = refs[-1]
        for i, off in enumerate(offsets):
            first_ref, second_ref = refs[i], refs[count + i]
            pick = _picker(me_ref[0], second_ref, capacity)
            place = lax.rem(me_ref[0] + (off + groups) % groups, groups)
            out_ref[place, :, :half] = jnp.dot(
                pick, first_ref[...], preferred_element_type=F32
            ).astype(BF)
            out_ref[place, :, half:] = jnp.dot(
                pick, second_ref[0:tokens, :], preferred_element_type=F32
            ).astype(BF)

    operands = list(firsts) + list(seconds) + ([] if rows is None else [rows])
    return pl.pallas_call(
        kernel,
        in_specs=[pl.BlockSpec(memory_space=pltpu.SMEM)]
        + [pl.BlockSpec(memory_space=pltpu.VMEM)] * len(operands)
        + [pl.BlockSpec(memory_space=pltpu.HBM)] * len(after),
        out_specs=pl.BlockSpec(memory_space=pltpu.VMEM),
        out_shape=jax.ShapeDtypeStruct(shape, BF),
        input_output_aliases={} if rows is None else {len(operands): 0},
        compiler_params=pltpu.CompilerParams(vmem_limit_bytes=VMEM),
        cost_estimate=pl.CostEstimate(
            flops=2 * count * capacity * tokens * width,
            bytes_accessed=2 * count * (tokens + capacity) * width,
            transcendentals=0,
        ),
        name=name,
    )(me, *operands, *after)


def _forward(me, step, block, info_block, rows, name):
    tokens = info_block.shape[0] - INFO_ROWS
    groups, capacity, _ = rows.shape
    width = block.shape[1]

    def kernel(me_ref, block_ref, info_ref, _, out_ref, __):
        expert = lax.rem(me_ref[0] + (step + groups) % groups, groups)
        pick = _picker(expert, info_ref, capacity)
        out_ref[...] = jnp.dot(
            pick, block_ref[0:tokens, :], preferred_element_type=F32
        ).astype(BF)

    return pl.pallas_call(
        kernel,
        in_specs=[pl.BlockSpec(memory_space=pltpu.SMEM)]
        + [pl.BlockSpec(memory_space=pltpu.VMEM)] * 3,
        out_specs=[pl.BlockSpec(memory_space=pltpu.VMEM)] * 2,
        out_shape=[
            jax.ShapeDtypeStruct((capacity, width), BF),
            jax.ShapeDtypeStruct(rows.shape, BF),
        ],
        input_output_aliases={3: 1},
        compiler_params=pltpu.CompilerParams(vmem_limit_bytes=VMEM),
        cost_estimate=pl.CostEstimate(
            flops=2 * capacity * tokens * width,
            bytes_accessed=2 * (tokens + capacity) * width,
            transcendentals=0,
        ),
        name=name,
    )(me, block, info_block, rows)


def _place(me, off, first, second, rows):
    groups, capacity, width = rows.shape
    half = width // 2

    def kernel(me_ref, first_ref, second_ref, _, out_ref):
        place = lax.rem(me_ref[0] + (off + groups) % groups, groups)
        out_ref[place, :, :half] = first_ref[...]
        out_ref[place, :, half:] = second_ref[...]

    return pl.pallas_call(
        kernel,
        in_specs=[pl.BlockSpec(memory_space=pltpu.SMEM)]
        + [pl.BlockSpec(memory_space=pltpu.VMEM)] * 3,
        out_specs=pl.BlockSpec(memory_space=pltpu.VMEM),
        out_shape=jax.ShapeDtypeStruct(rows.shape, BF),
        input_output_aliases={3: 0},
        compiler_params=pltpu.CompilerParams(vmem_limit_bytes=VMEM),
        cost_estimate=pl.CostEstimate(
            flops=0, bytes_accessed=4 * capacity * width, transcendentals=0
        ),
        name="place_last",
    )(me, first, second, rows)


def _copies(array, copies):
    def kernel(array_ref, out_ref):
        for i in range(copies):
            out_ref[i] = array_ref[...]

    return pl.pallas_call(
        kernel,
        in_specs=[pl.BlockSpec(memory_space=pltpu.VMEM)],
        out_specs=pl.BlockSpec(memory_space=pltpu.VMEM),
        out_shape=jax.ShapeDtypeStruct((copies,) + array.shape, BF),
        compiler_params=pltpu.CompilerParams(vmem_limit_bytes=VMEM),
        cost_estimate=pl.CostEstimate(
            flops=0, bytes_accessed=2 * (copies + 1) * array.size, transcendentals=0
        ),
        name="unit_copies",
    )(array)


def _term_kernel(saved_ref, rows_ref, out_ref):
    out_ref[...] = jnp.dot(saved_ref[...], rows_ref[...], preferred_element_type=F32).astype(BF)


def _term(saved_t, rows, name):
    units, depth = saved_t.shape
    width = rows.shape[1]
    block = 512 if width % 512 == 0 else LANES
    return pl.pallas_call(
        _term_kernel,
        grid=(width // block,),
        in_specs=[
            pl.BlockSpec((units, depth), lambda j: (0, 0)),
            pl.BlockSpec((depth, block), lambda j: (0, j)),
        ],
        out_specs=pl.BlockSpec((units, block), lambda j: (0, j)),
        out_shape=jax.ShapeDtypeStruct((units, width), BF),
        compiler_params=pltpu.CompilerParams(vmem_limit_bytes=VMEM),
        cost_estimate=pl.CostEstimate(
            flops=2 * units * depth * width,
            bytes_accessed=2 * (units * depth + depth * width + units * width),
            transcendentals=0,
        ),
        name=name,
    )(saved_t, rows)


def body(grads, routes, gates, hidden, down_weight):
    groups = lax.axis_size("expert")
    replicas = lax.axis_size("replica")
    chips = replicas // 2
    width = grads.shape[2]
    units_dev = down_weight.shape[0]
    rows_dev = hidden.shape[1]
    units = hidden.shape[2]
    capacity = rows_dev // groups
    half = width // 2
    me = lax.axis_index("expert").astype(jnp.int32).reshape(1)
    core = lax.rem(lax.axis_index("replica"), 2)

    chip_groups = [[2 * q + c for q in range(chips)] for c in range(2)]

    def over_chips(array):
        return lax.all_to_all(
            array, "replica", split_axis=0, concat_axis=0, tiled=True, axis_index_groups=chip_groups
        )

    def other_core(array):
        return lax.ppermute(array, "replica", [(i, i ^ 1) for i in range(replicas)])

    weights_mine = over_chips(_copies(down_weight[:, 0, :], chips))

    own_first, own_second = _pack(grads[0], routes.transpose(2, 0, 1), gates[0].T)

    up = [(i, (i + 1) % groups) for i in range(groups)]
    down = [(i, (i - 1) % groups) for i in range(groups)]
    far = groups // 2
    got_first, got_second = {0: own_first}, {0: own_second}
    a_up = a_down = own_first
    b_up = b_down = own_second
    rows = None
    shape = (groups, capacity, width)

    def pick(rows, batch, name, after=()):
        firsts = [got_first[off] for off in batch]
        seconds = [got_second[off] for off in batch]
        return _select(me, batch, firsts, seconds, rows, shape, name, after)

    saved_mine, saved_other = _split(hidden[0], core.reshape(1), units_dev)
    for hop in range(1, far):
        if hop == 2:
            b_up, saved_mine, saved_other = lax.optimization_barrier(
                (b_up, saved_mine, saved_other)
            )
        if hop >= 3:
            a_up, rows = lax.optimization_barrier((a_up, rows))
        a_up = lax.ppermute(a_up, "expert", up)
        a_down = lax.ppermute(a_down, "expert", down)
        b_up = lax.ppermute(b_up, "expert", up)
        b_down = lax.ppermute(b_down, "expert", down)
        got_first[-hop], got_second[hop] = a_up, b_down
        got_first[hop], got_second[-hop] = a_down, b_up
        if hop == 2:
            rows = pick(rows, [0, -1, 1], "select_1", (weights_mine,))
        elif hop >= 3:
            rows = pick(rows, [1 - hop, hop - 1], f"select_{hop - 1}")

    last_first, rows = _forward(me, 1, a_up, b_up, rows, "forward_up")
    last_first = lax.ppermute(last_first, "expert", up)
    last_second, rows = _forward(me, -1, b_down, b_down, rows, "forward_down")
    last_second = lax.ppermute(last_second, "expert", down)
    rows = pick(rows, [1 - far, far - 1], f"select_{far - 1}")
    rows = _place(me, far, last_first, last_second, rows)
    rows = rows.reshape(rows_dev, width)

    other = _term(saved_other, rows, "term_other")
    arrived = other_core(other)
    mine = _term(saved_mine, rows, "term_mine")
    pair = (mine.astype(F32) + arrived.astype(F32)).astype(BF)
    pair, rows, weights_mine = lax.optimization_barrier((pair, rows, weights_mine))
    sums = over_chips(pair.reshape(chips, units_dev, width))

    weights_other = other_core(weights_mine)
    both = jnp.where(
        core == 0,
        jnp.stack([weights_mine, weights_other], axis=1),
        jnp.stack([weights_other, weights_mine], axis=1),
    ).reshape(units, width)
    d_rows = lax.dot_general(rows, both, (((1,), (1,)), ((), ())), preferred_element_type=F32)
    d_hidden = d_rows.astype(BF)[None]
    sums, d_hidden = lax.optimization_barrier((sums, d_hidden))
    down_grad = jnp.sum(sums.astype(F32), axis=0)[:, None, :]
    return (d_hidden, down_grad)


def solution(mesh):
    placed = (P("replica", "expert", None),) * 5
    return jax.shard_map(
        body,
        mesh=mesh,
        in_specs=placed,
        out_specs=(P("replica", "expert", None), P("replica", "expert", None)),
        check_vma=False,
    )
```

```python
import jax
import jax.numpy as jnp
from jax import lax
from jax.experimental import pallas as pl
from jax.experimental.pallas import tpu as pltpu
from jax.sharding import PartitionSpec as P

BF = jnp.bfloat16
F32 = jnp.float32
LANES = 128
INFO_ROWS = 8
VMEM = 16 << 20


def _pack_kernel(grads_ref, routes_ref, gates_ref, first_ref, second_ref):
    top, _, tokens = routes_ref.shape
    half = first_ref.shape[1]
    experts = 2 * INFO_ROWS
    first_ref[...] = grads_ref[:, 0:half]
    second_ref[0:tokens, :] = grads_ref[:, half:]
    gates = gates_ref[...].astype(F32)
    expert = lax.broadcasted_iota(jnp.int32, (experts, tokens), 0)
    gate = jnp.zeros((experts, tokens), F32)
    named = jnp.zeros((experts, tokens), F32)
    for k in range(top):
        hit = routes_ref[k] == expert
        gate = jnp.where(hit, gates[k : k + 1, :], gate)
        named = jnp.where(hit, 1.0, named)
    row = lax.broadcasted_iota(jnp.int32, (tokens, tokens), 0)
    col = lax.broadcasted_iota(jnp.int32, (tokens, tokens), 1)
    earlier = jnp.where(row < col, 1.0, 0.0).astype(BF)
    rank = jnp.dot(named.astype(BF), earlier, preferred_element_type=F32)
    slot = jnp.where(named > 0.5, rank, -1.0)
    n = INFO_ROWS
    parts = [slot[0:n], gate[0:n], slot[n : 2 * n], gate[n : 2 * n]]
    parts.append(jnp.zeros((n, half - 4 * tokens), F32))
    second_ref[tokens : tokens + n, :] = jnp.concatenate(parts, axis=1).astype(BF)


def _pack(grads, routes_t, gates_t):
    tokens, width = grads.shape
    half = width // 2
    return pl.pallas_call(
        _pack_kernel,
        out_shape=[
            jax.ShapeDtypeStruct((tokens, half), BF),
            jax.ShapeDtypeStruct((tokens + INFO_ROWS, half), BF),
        ],
        compiler_params=pltpu.CompilerParams(vmem_limit_bytes=VMEM),
        cost_estimate=pl.CostEstimate(
            flops=1 << 20, bytes_accessed=4 * tokens * width, transcendentals=0
        ),
        name="pack_tokens",
    )(grads, routes_t, gates_t)


def _split_kernel(units_dev, core_ref, hidden_ref, _, mine_ref, other_ref):
    units = hidden_ref.shape[1]
    half = units // 2
    row = lax.broadcasted_iota(jnp.int32, (half, units), 0)
    col = lax.broadcasted_iota(jnp.int32, (half, units), 1)
    even = row + units_dev * (row // units_dev)
    for flip, out_ref in ((0, mine_ref), (1, other_ref)):
        core = lax.rem(core_ref[0] + flip, 2)
        pick = jnp.where(col == even + core * units_dev, 1.0, 0.0).astype(BF)
        out_ref[...] = lax.dot_general(
            pick, hidden_ref[...], (((1,), (1,)), ((), ())), preferred_element_type=F32
        ).astype(BF)


def _split(hidden, core, units_dev, after):
    rows, units = hidden.shape

    def kernel(*refs):
        _split_kernel(units_dev, *refs)

    return pl.pallas_call(
        kernel,
        in_specs=[
            pl.BlockSpec(memory_space=pltpu.SMEM),
            pl.BlockSpec(memory_space=pltpu.VMEM),
            pl.BlockSpec(memory_space=pl.ANY),
        ],
        out_specs=[pl.BlockSpec(memory_space=pltpu.VMEM)] * 2,
        out_shape=[jax.ShapeDtypeStruct((units // 2, rows), BF)] * 2,
        compiler_params=pltpu.CompilerParams(vmem_limit_bytes=VMEM),
        cost_estimate=pl.CostEstimate(
            flops=2 * rows * units * units, bytes_accessed=4 * rows * units, transcendentals=0
        ),
        name="split_hidden",
    )(core, hidden, after)


def _picker(expert, second_ref, capacity):
    tokens = second_ref.shape[0] - INFO_ROWS
    info = second_ref[tokens : tokens + INFO_ROWS, 0 : 4 * tokens].astype(F32)
    info = jnp.where(expert >= INFO_ROWS, info[:, 2 * tokens :], info[:, : 2 * tokens])
    row = lax.broadcasted_iota(jnp.int32, info.shape, 0)
    mine = jnp.sum(jnp.where(row == lax.rem(expert, INFO_ROWS), info, 0.0), axis=0, keepdims=True)
    slot = lax.broadcasted_iota(jnp.int32, (capacity, tokens), 0).astype(F32)
    return jnp.where(mine[:, :tokens] == slot, mine[:, tokens:], 0.0).astype(BF)


def _select(me, offsets, firsts, seconds, rows, shape, name, after=()):
    count = len(offsets)
    groups, capacity, width = shape
    half = width // 2
    tokens = firsts[0].shape[0]

    def kernel(me_ref, *refs):
        out_ref = refs[-1]
        for i, off in enumerate(offsets):
            first_ref, second_ref = refs[i], refs[count + i]
            pick = _picker(me_ref[0], second_ref, capacity)
            place = lax.rem(me_ref[0] + (off + groups) % groups, groups)
            out_ref[place, :, :half] = jnp.dot(
                pick, first_ref[...], preferred_element_type=F32
            ).astype(BF)
            out_ref[place, :, half:] = jnp.dot(
                pick, second_ref[0:tokens, :], preferred_element_type=F32
            ).astype(BF)

    operands = list(firsts) + list(seconds) + ([] if rows is None else [rows])
    return pl.pallas_call(
        kernel,
        in_specs=[pl.BlockSpec(memory_space=pltpu.SMEM)]
        + [pl.BlockSpec(memory_space=pltpu.VMEM)] * len(operands)
        + [pl.BlockSpec(memory_space=pltpu.HBM)] * len(after),
        out_specs=pl.BlockSpec(memory_space=pltpu.VMEM),
        out_shape=jax.ShapeDtypeStruct(shape, BF),
        input_output_aliases={} if rows is None else {len(operands): 0},
        compiler_params=pltpu.CompilerParams(vmem_limit_bytes=VMEM),
        cost_estimate=pl.CostEstimate(
            flops=2 * count * capacity * tokens * width,
            bytes_accessed=2 * count * (tokens + capacity) * width,
            transcendentals=0,
        ),
        name=name,
    )(me, *operands, *after)


def _forward(me, sends, first, second, rows, name, after=()):
    tokens = second.shape[0] - INFO_ROWS
    half = first.shape[1]
    groups, capacity, _ = rows.shape
    widths = [half * len(chunks) for _, chunks in sends]

    def kernel(me_ref, first_ref, second_ref, _, *refs):
        for (step, chunks), out_ref in zip(sends, refs[len(after) :]):
            expert = lax.rem(me_ref[0] + (step + groups) % groups, groups)
            pick = _picker(expert, second_ref, capacity)
            for n, chunk in enumerate(chunks):
                block_ref = (first_ref, second_ref)[chunk]
                out_ref[:, n * half : (n + 1) * half] = jnp.dot(
                    pick, block_ref[0:tokens, :], preferred_element_type=F32
                ).astype(BF)

    return pl.pallas_call(
        kernel,
        in_specs=[pl.BlockSpec(memory_space=pltpu.SMEM)]
        + [pl.BlockSpec(memory_space=pltpu.VMEM)] * 3
        + [pl.BlockSpec(memory_space=pl.ANY)] * len(after),
        out_specs=[pl.BlockSpec(memory_space=pltpu.VMEM)] * (len(sends) + 1),
        out_shape=[jax.ShapeDtypeStruct((capacity, w), BF) for w in widths]
        + [jax.ShapeDtypeStruct(rows.shape, BF)],
        input_output_aliases={3: len(sends)},
        compiler_params=pltpu.CompilerParams(vmem_limit_bytes=VMEM),
        cost_estimate=pl.CostEstimate(
            flops=2 * capacity * tokens * sum(widths),
            bytes_accessed=2 * (tokens + capacity) * sum(widths),
            transcendentals=0,
        ),
        name=name,
    )(me, first, second, rows, *after)


def _place(me, parts, rows, name):
    groups, capacity, _ = rows.shape
    count = len(parts)

    def kernel(me_ref, *refs):
        out_ref = refs[-1]
        for (off, column, part), part_ref in zip(parts, refs):
            place = lax.rem(me_ref[0] + (off + groups) % groups, groups)
            out_ref[place, :, column : column + part.shape[1]] = part_ref[...]

    arrays = [part for _, _, part in parts]
    return pl.pallas_call(
        kernel,
        in_specs=[pl.BlockSpec(memory_space=pltpu.SMEM)]
        + [pl.BlockSpec(memory_space=pltpu.VMEM)] * (count + 1),
        out_specs=pl.BlockSpec(memory_space=pltpu.VMEM),
        out_shape=jax.ShapeDtypeStruct(rows.shape, BF),
        input_output_aliases={count + 1: 0},
        compiler_params=pltpu.CompilerParams(vmem_limit_bytes=VMEM),
        cost_estimate=pl.CostEstimate(
            flops=0, bytes_accessed=4 * sum(a.size for a in arrays), transcendentals=0
        ),
        name=name,
    )(me, *arrays, rows)


def _copies(array, copies):
    def kernel(array_ref, out_ref):
        for i in range(copies):
            out_ref[i] = array_ref[...]

    return pl.pallas_call(
        kernel,
        in_specs=[pl.BlockSpec(memory_space=pltpu.VMEM)],
        out_specs=pl.BlockSpec(memory_space=pltpu.VMEM),
        out_shape=jax.ShapeDtypeStruct((copies,) + array.shape, BF),
        compiler_params=pltpu.CompilerParams(vmem_limit_bytes=VMEM),
        cost_estimate=pl.CostEstimate(
            flops=0, bytes_accessed=2 * (copies + 1) * array.size, transcendentals=0
        ),
        name="unit_copies",
    )(array)


def _once(array, after):
    def kernel(*_):
        pass

    return pl.pallas_call(
        kernel,
        in_specs=[pl.BlockSpec(memory_space=pltpu.HBM), pl.BlockSpec(memory_space=pl.ANY)],
        out_specs=pl.BlockSpec(memory_space=pltpu.HBM),
        out_shape=pltpu.HBM(array.shape, BF),
        input_output_aliases={0: 0},
        cost_estimate=pl.CostEstimate(flops=0, bytes_accessed=0, transcendentals=0),
        name="once",
    )(array, after)


def _sum_kernel(parts_ref, out_ref):
    total = parts_ref[0].astype(F32)
    for i in range(1, parts_ref.shape[0]):
        total += parts_ref[i].astype(F32)
    for i in range(total.shape[0]):
        out_ref[i, :, :] = total[i : i + 1, :]


def _sum(parts):
    chips, units, width = parts.shape
    block = 512 if width % 512 == 0 else LANES
    return pl.pallas_call(
        _sum_kernel,
        grid=(width // block,),
        in_specs=[pl.BlockSpec((chips, units, block), lambda j: (0, 0, j))],
        out_specs=pl.BlockSpec((units, 1, block), lambda j: (0, 0, j)),
        out_shape=jax.ShapeDtypeStruct((units, 1, width), F32),
        compiler_params=pltpu.CompilerParams(vmem_limit_bytes=VMEM),
        cost_estimate=pl.CostEstimate(
            flops=parts.size, bytes_accessed=2 * parts.size, transcendentals=0
        ),
        name="sum_parts",
    )(parts)


def _term_kernel(saved_ref, rows_ref, out_ref):
    out_ref[...] = jnp.dot(saved_ref[...], rows_ref[...], preferred_element_type=F32).astype(BF)


def _term(saved_t, rows, name):
    units, depth = saved_t.shape
    width = rows.shape[1]
    block = 512 if width % 512 == 0 else LANES
    return pl.pallas_call(
        _term_kernel,
        grid=(width // block,),
        in_specs=[
            pl.BlockSpec((units, depth), lambda j: (0, 0)),
            pl.BlockSpec((depth, block), lambda j: (0, j)),
        ],
        out_specs=pl.BlockSpec((units, block), lambda j: (0, j)),
        out_shape=jax.ShapeDtypeStruct((units, width), BF),
        compiler_params=pltpu.CompilerParams(vmem_limit_bytes=VMEM),
        cost_estimate=pl.CostEstimate(
            flops=2 * units * depth * width,
            bytes_accessed=2 * (units * depth + depth * width + units * width),
            transcendentals=0,
        ),
        name=name,
    )(saved_t, rows)


def body(grads, routes, gates, hidden, down_weight):
    groups = lax.axis_size("expert")
    replicas = lax.axis_size("replica")
    chips = replicas // 2
    width = grads.shape[2]
    units_dev = down_weight.shape[0]
    rows_dev = hidden.shape[1]
    units = hidden.shape[2]
    capacity = rows_dev // groups
    half = width // 2
    me = lax.axis_index("expert").astype(jnp.int32).reshape(1)
    core = lax.rem(lax.axis_index("replica"), 2)

    chip_groups = [[2 * q + c for q in range(chips)] for c in range(2)]

    def over_chips(array):
        return lax.all_to_all(
            array, "replica", split_axis=0, concat_axis=0, tiled=True, axis_index_groups=chip_groups
        )

    def other_core(array):
        return lax.ppermute(array, "replica", [(i, i ^ 1) for i in range(replicas)])

    weights_mine = over_chips(_copies(down_weight[:, 0, :], chips))

    own_first, own_second = _pack(grads[0], routes.transpose(2, 0, 1), gates[0].T)

    far = groups // 2
    relay = far - 3

    def shift(array, places):
        return lax.ppermute(array, "expert", [(i, (i + places) % groups) for i in range(groups)])

    got_first, got_second = {0: own_first}, {0: own_second}
    a_up = a_down = own_first
    b_up = b_down = own_second
    rows = None
    shape = (groups, capacity, width)

    def pick(rows, batch, name, after=()):
        firsts = [got_first[off] for off in batch]
        seconds = [got_second[off] for off in batch]
        return _select(me, batch, firsts, seconds, rows, shape, name, after)

    saved_mine, saved_other = _split(hidden[0], core.reshape(1), units_dev, own_first)
    for hop in range(1, relay + 1):
        if hop == 2:
            b_up, saved_mine, saved_other = lax.optimization_barrier(
                (b_up, saved_mine, saved_other)
            )
        if hop >= 3:
            a_up, rows = lax.optimization_barrier((a_up, rows))
        a_up, a_down = shift(a_up, 1), shift(a_down, -1)
        b_up, b_down = shift(b_up, 1), shift(b_down, -1)
        got_first[-hop], got_first[hop] = a_up, a_down
        got_second[-hop], got_second[hop] = b_up, b_down
        if hop == 2:
            rows = pick(rows, [0, -1, 1], "select_1", (weights_mine,))
        elif hop >= 3:
            rows = pick(rows, [1 - hop, hop - 1], f"select_{hop - 1}")

    far_down, rows = _forward(me, [(-3, (1,))], b_down, b_down, rows, "forward_far")
    far_down = shift(far_down, -3)
    up_2, up_3, up_1, rows = _forward(
        me, [(2, (0, 1)), (3, (0,)), (1, (0, 1))], a_up, b_up, rows, "forward_up"
    )
    down_2, down_1, rows = _forward(
        me, [(-2, (0, 1)), (-1, (0, 1))], a_down, b_down, rows, "forward_down"
    )
    rows = pick(rows, [-relay, relay], f"select_{relay}")
    up_2, down_2, far_up = shift(up_2, 2), shift(down_2, -2), shift(up_3, 3)
    up_1, down_1 = shift(up_1, 1), shift(down_1, -1)
    parts = [(-relay - 2, 0, up_2), (relay + 2, 0, down_2), (far, 0, far_up), (far, half, far_down)]
    rows = _place(me, parts, rows, "place_far")
    rows = _place(me, [(-relay - 1, 0, up_1), (relay + 1, 0, down_1)], rows, "place_near")
    rows = rows.reshape(rows_dev, width)

    other = _term(saved_other, rows, "term_other")
    arrived = other_core(other)
    mine = _term(saved_mine, rows, "term_mine")
    pair = (mine.astype(F32) + arrived.astype(F32)).astype(BF)
    pair, rows = lax.optimization_barrier((pair, rows))
    sums = over_chips(pair.reshape(chips, units_dev, width))

    weights_other = other_core(weights_mine)
    both = jnp.where(
        core == 0,
        jnp.stack([weights_mine, weights_other], axis=1),
        jnp.stack([weights_other, weights_mine], axis=1),
    ).reshape(units, width)
    d_rows = lax.dot_general(rows, both, (((1,), (1,)), ((), ())), preferred_element_type=F32)
    d_hidden = d_rows.astype(BF)[None]
    sums, d_hidden = lax.optimization_barrier((sums, d_hidden))
    down_grad = _sum(sums)
    return (d_hidden, down_grad)


def solution(mesh):
    placed = (P("replica", "expert", None),) * 5
    return jax.shard_map(
        body,
        mesh=mesh,
        in_specs=placed,
        out_specs=(P("replica", "expert", None), P("replica", "expert", None)),
        check_vma=False,
    )
```

```python
import jax
import jax.numpy as jnp
from jax import lax
from jax.experimental import pallas as pl
from jax.experimental.pallas import tpu as pltpu
from jax.sharding import PartitionSpec as P

BF = jnp.bfloat16
F32 = jnp.float32
LANES = 128
INFO_ROWS = 8
VMEM = 16 << 20


def _pack_kernel(grads_ref, routes_ref, gates_ref, first_ref, second_ref):
    top, _, tokens = routes_ref.shape
    half = first_ref.shape[1]
    experts = 2 * INFO_ROWS
    first_ref[...] = grads_ref[:, 0:half]
    second_ref[0:tokens, :] = grads_ref[:, half:]
    gates = gates_ref[...].astype(F32)
    expert = lax.broadcasted_iota(jnp.int32, (experts, tokens), 0)
    gate = jnp.zeros((experts, tokens), F32)
    named = jnp.zeros((experts, tokens), F32)
    for k in range(top):
        hit = routes_ref[k] == expert
        gate = jnp.where(hit, gates[k : k + 1, :], gate)
        named = jnp.where(hit, 1.0, named)
    row = lax.broadcasted_iota(jnp.int32, (tokens, tokens), 0)
    col = lax.broadcasted_iota(jnp.int32, (tokens, tokens), 1)
    earlier = jnp.where(row < col, 1.0, 0.0).astype(BF)
    rank = jnp.dot(named.astype(BF), earlier, preferred_element_type=F32)
    slot = jnp.where(named > 0.5, rank, -1.0)
    n = INFO_ROWS
    parts = [slot[0:n], gate[0:n], slot[n : 2 * n], gate[n : 2 * n]]
    parts.append(jnp.zeros((n, half - 4 * tokens), F32))
    second_ref[tokens : tokens + n, :] = jnp.concatenate(parts, axis=1).astype(BF)


def _pack(grads, routes_t, gates_t):
    tokens, width = grads.shape
    half = width // 2
    return pl.pallas_call(
        _pack_kernel,
        out_shape=[
            jax.ShapeDtypeStruct((tokens, half), BF),
            jax.ShapeDtypeStruct((tokens + INFO_ROWS, half), BF),
        ],
        compiler_params=pltpu.CompilerParams(vmem_limit_bytes=VMEM),
        cost_estimate=pl.CostEstimate(
            flops=1 << 20, bytes_accessed=4 * tokens * width, transcendentals=0
        ),
        name="pack_tokens",
    )(grads, routes_t, gates_t)


def _split_kernel(units_dev, core_ref, hidden_ref, _, mine_ref, other_ref):
    units = hidden_ref.shape[1]
    half = units // 2
    row = lax.broadcasted_iota(jnp.int32, (half, units), 0)
    col = lax.broadcasted_iota(jnp.int32, (half, units), 1)
    even = row + units_dev * (row // units_dev)
    for flip, out_ref in ((0, mine_ref), (1, other_ref)):
        core = lax.rem(core_ref[0] + flip, 2)
        pick = jnp.where(col == even + core * units_dev, 1.0, 0.0).astype(BF)
        out_ref[...] = lax.dot_general(
            pick, hidden_ref[...], (((1,), (1,)), ((), ())), preferred_element_type=F32
        ).astype(BF)


def _split(hidden, core, units_dev, after):
    rows, units = hidden.shape

    def kernel(*refs):
        _split_kernel(units_dev, *refs)

    return pl.pallas_call(
        kernel,
        in_specs=[
            pl.BlockSpec(memory_space=pltpu.SMEM),
            pl.BlockSpec(memory_space=pltpu.VMEM),
            pl.BlockSpec(memory_space=pl.ANY),
        ],
        out_specs=[pl.BlockSpec(memory_space=pltpu.VMEM)] * 2,
        out_shape=[jax.ShapeDtypeStruct((units // 2, rows), BF)] * 2,
        compiler_params=pltpu.CompilerParams(vmem_limit_bytes=VMEM),
        cost_estimate=pl.CostEstimate(
            flops=2 * rows * units * units, bytes_accessed=4 * rows * units, transcendentals=0
        ),
        name="split_hidden",
    )(core, hidden, after)


def _picker(expert, second_ref, capacity):
    tokens = second_ref.shape[0] - INFO_ROWS
    info = second_ref[tokens : tokens + INFO_ROWS, 0 : 4 * tokens].astype(F32)
    info = jnp.where(expert >= INFO_ROWS, info[:, 2 * tokens :], info[:, : 2 * tokens])
    row = lax.broadcasted_iota(jnp.int32, info.shape, 0)
    mine = jnp.sum(jnp.where(row == lax.rem(expert, INFO_ROWS), info, 0.0), axis=0, keepdims=True)
    slot = lax.broadcasted_iota(jnp.int32, (capacity, tokens), 0).astype(F32)
    return jnp.where(mine[:, :tokens] == slot, mine[:, tokens:], 0.0).astype(BF)


def _select(me, offsets, firsts, seconds, rows, shape, name, after=()):
    count = len(offsets)
    groups, capacity, width = shape
    half = width // 2
    tokens = firsts[0].shape[0]

    def kernel(me_ref, *refs):
        out_ref = refs[-1]
        for i, off in enumerate(offsets):
            first_ref, second_ref = refs[i], refs[count + i]
            pick = _picker(me_ref[0], second_ref, capacity)
            place = lax.rem(me_ref[0] + (off + groups) % groups, groups)
            out_ref[place, :, :half] = jnp.dot(
                pick, first_ref[...], preferred_element_type=F32
            ).astype(BF)
            out_ref[place, :, half:] = jnp.dot(
                pick, second_ref[0:tokens, :], preferred_element_type=F32
            ).astype(BF)

    operands = list(firsts) + list(seconds) + ([] if rows is None else [rows])
    return pl.pallas_call(
        kernel,
        in_specs=[pl.BlockSpec(memory_space=pltpu.SMEM)]
        + [pl.BlockSpec(memory_space=pltpu.VMEM)] * len(operands)
        + [pl.BlockSpec(memory_space=pltpu.HBM)] * len(after),
        out_specs=pl.BlockSpec(memory_space=pltpu.VMEM),
        out_shape=jax.ShapeDtypeStruct(shape, BF),
        input_output_aliases={} if rows is None else {len(operands): 0},
        compiler_params=pltpu.CompilerParams(vmem_limit_bytes=VMEM),
        cost_estimate=pl.CostEstimate(
            flops=2 * count * capacity * tokens * width,
            bytes_accessed=2 * count * (tokens + capacity) * width,
            transcendentals=0,
        ),
        name=name,
    )(me, *operands, *after)


def _forward(me, sends, first, second, rows, name, after=()):
    tokens = second.shape[0] - INFO_ROWS
    half = first.shape[1]
    groups, capacity, _ = rows.shape
    widths = [half * len(chunks) for _, chunks in sends]

    def kernel(me_ref, first_ref, second_ref, _, *refs):
        for (step, chunks), out_ref in zip(sends, refs[len(after) :]):
            expert = lax.rem(me_ref[0] + (step + groups) % groups, groups)
            pick = _picker(expert, second_ref, capacity)
            for n, chunk in enumerate(chunks):
                block_ref = (first_ref, second_ref)[chunk]
                out_ref[:, n * half : (n + 1) * half] = jnp.dot(
                    pick, block_ref[0:tokens, :], preferred_element_type=F32
                ).astype(BF)

    return pl.pallas_call(
        kernel,
        in_specs=[pl.BlockSpec(memory_space=pltpu.SMEM)]
        + [pl.BlockSpec(memory_space=pltpu.VMEM)] * 3
        + [pl.BlockSpec(memory_space=pl.ANY)] * len(after),
        out_specs=[pl.BlockSpec(memory_space=pltpu.VMEM)] * (len(sends) + 1),
        out_shape=[jax.ShapeDtypeStruct((capacity, w), BF) for w in widths]
        + [jax.ShapeDtypeStruct(rows.shape, BF)],
        input_output_aliases={3: len(sends)},
        compiler_params=pltpu.CompilerParams(vmem_limit_bytes=VMEM),
        cost_estimate=pl.CostEstimate(
            flops=2 * capacity * tokens * sum(widths),
            bytes_accessed=2 * (tokens + capacity) * sum(widths),
            transcendentals=0,
        ),
        name=name,
    )(me, first, second, rows, *after)


def _place(me, parts, rows, name):
    groups, capacity, _ = rows.shape
    count = len(parts)

    def kernel(me_ref, *refs):
        out_ref = refs[-1]
        for (off, column, part), part_ref in zip(parts, refs):
            place = lax.rem(me_ref[0] + (off + groups) % groups, groups)
            out_ref[place, :, column : column + part.shape[1]] = part_ref[...]

    arrays = [part for _, _, part in parts]
    return pl.pallas_call(
        kernel,
        in_specs=[pl.BlockSpec(memory_space=pltpu.SMEM)]
        + [pl.BlockSpec(memory_space=pltpu.VMEM)] * (count + 1),
        out_specs=pl.BlockSpec(memory_space=pltpu.VMEM),
        out_shape=jax.ShapeDtypeStruct(rows.shape, BF),
        input_output_aliases={count + 1: 0},
        compiler_params=pltpu.CompilerParams(vmem_limit_bytes=VMEM),
        cost_estimate=pl.CostEstimate(
            flops=0, bytes_accessed=4 * sum(a.size for a in arrays), transcendentals=0
        ),
        name=name,
    )(me, *arrays, rows)


def _copies(array, copies):
    def kernel(array_ref, out_ref, sems):
        started = []
        for i in range(copies):
            started.append(pltpu.make_async_copy(array_ref, out_ref.at[i], sems.at[i]))
            started[-1].start()
        for copy in started:
            copy.wait()

    return pl.pallas_call(
        kernel,
        in_specs=[pl.BlockSpec(memory_space=pltpu.VMEM)],
        out_specs=pl.BlockSpec(memory_space=pltpu.HBM),
        out_shape=pltpu.HBM((copies,) + array.shape, BF),
        scratch_shapes=[pltpu.SemaphoreType.DMA((copies,))],
        compiler_params=pltpu.CompilerParams(vmem_limit_bytes=VMEM),
        cost_estimate=pl.CostEstimate(
            flops=0, bytes_accessed=2 * (copies + 1) * array.size, transcendentals=0
        ),
        name="unit_copies",
    )(array)


def _term(saved_t, rows, name, more=None):
    units, depth = saved_t.shape
    width = rows.shape[1]
    block = 512 if width % 512 == 0 else LANES

    def kernel(saved_ref, rows_ref, *refs):
        columns = pl.ds(pl.multiple_of(pl.program_id(0) * block, block), block)
        term = jnp.dot(saved_ref[...], rows_ref[:, columns], preferred_element_type=F32).astype(BF)
        if more is not None:
            term = (term.astype(F32) + refs[0][:, columns].astype(F32)).astype(BF)
        refs[-1][...] = term

    operands = [saved_t, rows] + ([] if more is None else [more])
    return pl.pallas_call(
        kernel,
        grid=(width // block,),
        in_specs=[pl.BlockSpec(memory_space=pltpu.VMEM)] * len(operands),
        out_specs=pl.BlockSpec((units, block), lambda j: (0, j)),
        out_shape=jax.ShapeDtypeStruct((units, width), BF)
        if more is None
        else pltpu.HBM((units, width), BF),
        compiler_params=pltpu.CompilerParams(vmem_limit_bytes=VMEM),
        cost_estimate=pl.CostEstimate(
            flops=2 * units * depth * width,
            bytes_accessed=2 * (units * depth + depth * width + units * width),
            transcendentals=0,
        ),
        name=name,
    )(*operands)


def body(grads, routes, gates, hidden, down_weight):
    groups = lax.axis_size("expert")
    replicas = lax.axis_size("replica")
    chips = replicas // 2
    width = grads.shape[2]
    units_dev = down_weight.shape[0]
    rows_dev = hidden.shape[1]
    units = hidden.shape[2]
    capacity = rows_dev // groups
    half = width // 2
    me = lax.axis_index("expert").astype(jnp.int32).reshape(1)
    core = lax.rem(lax.axis_index("replica"), 2)

    chip_groups = [[2 * q + c for q in range(chips)] for c in range(2)]

    def over_chips(array):
        return lax.all_to_all(
            array, "replica", split_axis=0, concat_axis=0, tiled=True, axis_index_groups=chip_groups
        )

    def other_core(array):
        return lax.ppermute(array, "replica", [(i, i ^ 1) for i in range(replicas)])

    weights_mine = over_chips(_copies(down_weight[:, 0, :], chips))

    own_first, own_second = _pack(grads[0], routes.transpose(2, 0, 1), gates[0].T)

    far = groups // 2
    relay = far - 3

    def shift(array, places):
        return lax.ppermute(array, "expert", [(i, (i + places) % groups) for i in range(groups)])

    got_first, got_second = {0: own_first}, {0: own_second}
    a_up = a_down = own_first
    b_up = b_down = own_second
    rows = None
    shape = (groups, capacity, width)

    def pick(rows, batch, name, after=()):
        firsts = [got_first[off] for off in batch]
        seconds = [got_second[off] for off in batch]
        return _select(me, batch, firsts, seconds, rows, shape, name, after)

    saved_mine, saved_other = _split(hidden[0], core.reshape(1), units_dev, own_first)
    for hop in range(1, relay + 1):
        if hop == 2:
            b_up, saved_mine, saved_other = lax.optimization_barrier(
                (b_up, saved_mine, saved_other)
            )
        if hop >= 3:
            a_up, rows = lax.optimization_barrier((a_up, rows))
        a_up, a_down = shift(a_up, 1), shift(a_down, -1)
        b_up, b_down = shift(b_up, 1), shift(b_down, -1)
        got_first[-hop], got_first[hop] = a_up, a_down
        got_second[-hop], got_second[hop] = b_up, b_down
        if hop == 2:
            rows = pick(rows, [0, -1, 1], "select_1", (weights_mine,))
        elif hop >= 3:
            rows = pick(rows, [1 - hop, hop - 1], f"select_{hop - 1}")

    far_down, rows = _forward(me, [(-3, (1,))], b_down, b_down, rows, "forward_far")
    far_down = shift(far_down, -3)
    up_2, up_3, up_1, rows = _forward(
        me, [(2, (0, 1)), (3, (0,)), (1, (0, 1))], a_up, b_up, rows, "forward_up"
    )
    down_2, down_1, rows = _forward(
        me, [(-2, (0, 1)), (-1, (0, 1))], a_down, b_down, rows, "forward_down"
    )
    rows = pick(rows, [-relay, relay], f"select_{relay}")
    up_2, down_2, far_up = shift(up_2, 2), shift(down_2, -2), shift(up_3, 3)
    up_1, down_1 = shift(up_1, 1), shift(down_1, -1)
    parts = [(-relay - 2, 0, up_2), (relay + 2, 0, down_2), (far, half, far_down)]
    rows = _place(me, parts, rows, "place_early")
    parts = [(-relay - 1, 0, up_1), (relay + 1, 0, down_1), (far, 0, far_up)]
    rows = _place(me, parts, rows, "place_late")
    rows = rows.reshape(rows_dev, width)

    other = _term(saved_other, rows, "term_other")
    arrived = other_core(other)
    pair = _term(saved_mine, rows, "term_pair", arrived)
    pair, rows = lax.optimization_barrier((pair, rows))
    sums = over_chips(pair.reshape(chips, units_dev, width))

    weights_other = other_core(weights_mine)
    both = jnp.where(
        core == 0,
        jnp.stack([weights_mine, weights_other], axis=1),
        jnp.stack([weights_other, weights_mine], axis=1),
    ).reshape(units, width)
    d_rows = lax.dot_general(rows, both, (((1,), (1,)), ((), ())), preferred_element_type=F32)
    d_hidden = d_rows.astype(BF)[None]
    sums, d_hidden = lax.optimization_barrier((sums, d_hidden))
    down_grad = jnp.sum(sums.astype(F32), axis=0)[:, None, :]
    return (d_hidden, down_grad)


def solution(mesh):
    placed = (P("replica", "expert", None),) * 5
    return jax.shard_map(
        body,
        mesh=mesh,
        in_specs=placed,
        out_specs=(P("replica", "expert", None), P("replica", "expert", None)),
        check_vma=False,
    )
```

```python
import jax
import jax.numpy as jnp
from jax import lax
from jax.experimental import pallas as pl
from jax.experimental.pallas import tpu as pltpu
from jax.sharding import PartitionSpec as P

BF = jnp.bfloat16
F32 = jnp.float32
LANES = 128
INFO_ROWS = 8
VMEM = 16 << 20


def _pack_kernel(grads_ref, routes_ref, gates_ref, first_ref, second_ref):
    top, _, tokens = routes_ref.shape
    half = first_ref.shape[1]
    experts = 2 * INFO_ROWS
    first_ref[...] = grads_ref[:, 0:half]
    second_ref[0:tokens, :] = grads_ref[:, half:]
    gates = gates_ref[...].astype(F32)
    expert = lax.broadcasted_iota(jnp.int32, (experts, tokens), 0)
    gate = jnp.zeros((experts, tokens), F32)
    named = jnp.zeros((experts, tokens), F32)
    for k in range(top):
        hit = routes_ref[k] == expert
        gate = jnp.where(hit, gates[k : k + 1, :], gate)
        named = jnp.where(hit, 1.0, named)
    row = lax.broadcasted_iota(jnp.int32, (tokens, tokens), 0)
    col = lax.broadcasted_iota(jnp.int32, (tokens, tokens), 1)
    earlier = jnp.where(row < col, 1.0, 0.0).astype(BF)
    rank = jnp.dot(named.astype(BF), earlier, preferred_element_type=F32)
    slot = jnp.where(named > 0.5, rank, -1.0)
    n = INFO_ROWS
    parts = [slot[0:n], gate[0:n], slot[n : 2 * n], gate[n : 2 * n]]
    parts.append(jnp.zeros((n, half - 4 * tokens), F32))
    second_ref[tokens : tokens + n, :] = jnp.concatenate(parts, axis=1).astype(BF)


def _pack(grads, routes_t, gates_t):
    tokens, width = grads.shape
    half = width // 2
    return pl.pallas_call(
        _pack_kernel,
        out_shape=[
            jax.ShapeDtypeStruct((tokens, half), BF),
            jax.ShapeDtypeStruct((tokens + INFO_ROWS, half), BF),
        ],
        compiler_params=pltpu.CompilerParams(vmem_limit_bytes=VMEM),
        cost_estimate=pl.CostEstimate(
            flops=1 << 20, bytes_accessed=4 * tokens * width, transcendentals=0
        ),
        name="pack_tokens",
    )(grads, routes_t, gates_t)


def _split_kernel(units_dev, core_ref, hidden_ref, _, mine_ref, other_ref):
    units = hidden_ref.shape[1]
    half = units // 2
    row = lax.broadcasted_iota(jnp.int32, (half, units), 0)
    col = lax.broadcasted_iota(jnp.int32, (half, units), 1)
    even = row + units_dev * (row // units_dev)
    for flip, out_ref in ((0, mine_ref), (1, other_ref)):
        core = lax.rem(core_ref[0] + flip, 2)
        pick = jnp.where(col == even + core * units_dev, 1.0, 0.0).astype(BF)
        out_ref[...] = lax.dot_general(
            pick, hidden_ref[...], (((1,), (1,)), ((), ())), preferred_element_type=F32
        ).astype(BF)


def _split(hidden, core, units_dev, after):
    rows, units = hidden.shape

    def kernel(*refs):
        _split_kernel(units_dev, *refs)

    return pl.pallas_call(
        kernel,
        in_specs=[
            pl.BlockSpec(memory_space=pltpu.SMEM),
            pl.BlockSpec(memory_space=pltpu.VMEM),
            pl.BlockSpec(memory_space=pl.ANY),
        ],
        out_specs=[pl.BlockSpec(memory_space=pltpu.VMEM)] * 2,
        out_shape=[jax.ShapeDtypeStruct((units // 2, rows), BF)] * 2,
        compiler_params=pltpu.CompilerParams(vmem_limit_bytes=VMEM),
        cost_estimate=pl.CostEstimate(
            flops=2 * rows * units * units, bytes_accessed=4 * rows * units, transcendentals=0
        ),
        name="split_hidden",
    )(core, hidden, after)


def _picker(expert, second_ref, capacity):
    tokens = second_ref.shape[0] - INFO_ROWS
    info = second_ref[tokens : tokens + INFO_ROWS, 0 : 4 * tokens].astype(F32)
    info = jnp.where(expert >= INFO_ROWS, info[:, 2 * tokens :], info[:, : 2 * tokens])
    row = lax.broadcasted_iota(jnp.int32, info.shape, 0)
    mine = jnp.sum(jnp.where(row == lax.rem(expert, INFO_ROWS), info, 0.0), axis=0, keepdims=True)
    slot = lax.broadcasted_iota(jnp.int32, (capacity, tokens), 0).astype(F32)
    return jnp.where(mine[:, :tokens] == slot, mine[:, tokens:], 0.0).astype(BF)


def _select(me, offsets, firsts, seconds, rows, shape, name, after=()):
    count = len(offsets)
    groups, capacity, width = shape
    half = width // 2
    tokens = firsts[0].shape[0]

    def kernel(me_ref, *refs):
        out_ref = refs[-1]
        for i, off in enumerate(offsets):
            first_ref, second_ref = refs[i], refs[count + i]
            pick = _picker(me_ref[0], second_ref, capacity)
            place = lax.rem(me_ref[0] + (off + groups) % groups, groups)
            out_ref[place, :, :half] = jnp.dot(
                pick, first_ref[...], preferred_element_type=F32
            ).astype(BF)
            out_ref[place, :, half:] = jnp.dot(
                pick, second_ref[0:tokens, :], preferred_element_type=F32
            ).astype(BF)

    operands = list(firsts) + list(seconds) + ([] if rows is None else [rows])
    return pl.pallas_call(
        kernel,
        in_specs=[pl.BlockSpec(memory_space=pltpu.SMEM)]
        + [pl.BlockSpec(memory_space=pltpu.VMEM)] * len(operands)
        + [pl.BlockSpec(memory_space=pltpu.HBM)] * len(after),
        out_specs=pl.BlockSpec(memory_space=pltpu.VMEM),
        out_shape=jax.ShapeDtypeStruct(shape, BF),
        input_output_aliases={} if rows is None else {len(operands): 0},
        compiler_params=pltpu.CompilerParams(vmem_limit_bytes=VMEM),
        cost_estimate=pl.CostEstimate(
            flops=2 * count * capacity * tokens * width,
            bytes_accessed=2 * count * (tokens + capacity) * width,
            transcendentals=0,
        ),
        name=name,
    )(me, *operands, *after)


def _forward(me, sends, first, second, rows, name, after=()):
    tokens = second.shape[0] - INFO_ROWS
    half = first.shape[1]
    groups, capacity, _ = rows.shape
    widths = [half * len(chunks) for _, chunks in sends]

    def kernel(me_ref, first_ref, second_ref, _, *refs):
        for (step, chunks), out_ref in zip(sends, refs[len(after) :]):
            expert = lax.rem(me_ref[0] + (step + groups) % groups, groups)
            pick = _picker(expert, second_ref, capacity)
            for n, chunk in enumerate(chunks):
                block_ref = (first_ref, second_ref)[chunk]
                out_ref[:, n * half : (n + 1) * half] = jnp.dot(
                    pick, block_ref[0:tokens, :], preferred_element_type=F32
                ).astype(BF)

    return pl.pallas_call(
        kernel,
        in_specs=[pl.BlockSpec(memory_space=pltpu.SMEM)]
        + [pl.BlockSpec(memory_space=pltpu.VMEM)] * 3
        + [pl.BlockSpec(memory_space=pl.ANY)] * len(after),
        out_specs=[pl.BlockSpec(memory_space=pltpu.VMEM)] * (len(sends) + 1),
        out_shape=[jax.ShapeDtypeStruct((capacity, w), BF) for w in widths]
        + [jax.ShapeDtypeStruct(rows.shape, BF)],
        input_output_aliases={3: len(sends)},
        compiler_params=pltpu.CompilerParams(vmem_limit_bytes=VMEM),
        cost_estimate=pl.CostEstimate(
            flops=2 * capacity * tokens * sum(widths),
            bytes_accessed=2 * (tokens + capacity) * sum(widths),
            transcendentals=0,
        ),
        name=name,
    )(me, first, second, rows, *after)


def _place(me, parts, rows, name):
    groups, capacity, _ = rows.shape
    count = len(parts)

    def kernel(me_ref, *refs):
        out_ref = refs[-1]
        for (off, column, part), part_ref in zip(parts, refs):
            place = lax.rem(me_ref[0] + (off + groups) % groups, groups)
            out_ref[place, :, column : column + part.shape[1]] = part_ref[...]

    arrays = [part for _, _, part in parts]
    return pl.pallas_call(
        kernel,
        in_specs=[pl.BlockSpec(memory_space=pltpu.SMEM)]
        + [pl.BlockSpec(memory_space=pltpu.VMEM)] * (count + 1),
        out_specs=pl.BlockSpec(memory_space=pltpu.VMEM),
        out_shape=jax.ShapeDtypeStruct(rows.shape, BF),
        input_output_aliases={count + 1: 0},
        compiler_params=pltpu.CompilerParams(vmem_limit_bytes=VMEM),
        cost_estimate=pl.CostEstimate(
            flops=0, bytes_accessed=4 * sum(a.size for a in arrays), transcendentals=0
        ),
        name=name,
    )(me, *arrays, rows)


def _copies(array, copies):
    def kernel(array_ref, out_ref, sems):
        started = []
        for i in range(copies):
            started.append(pltpu.make_async_copy(array_ref, out_ref.at[i], sems.at[i]))
            started[-1].start()
        for copy in started:
            copy.wait()

    return pl.pallas_call(
        kernel,
        in_specs=[pl.BlockSpec(memory_space=pltpu.HBM)],
        out_specs=pl.BlockSpec(memory_space=pltpu.HBM),
        out_shape=pltpu.HBM((copies,) + array.shape, BF),
        scratch_shapes=[pltpu.SemaphoreType.DMA((copies,))],
        compiler_params=pltpu.CompilerParams(vmem_limit_bytes=VMEM),
        cost_estimate=pl.CostEstimate(
            flops=0, bytes_accessed=2 * (copies + 1) * array.size, transcendentals=0
        ),
        name="unit_copies",
    )(array)


def _term(saved_t, rows, name, more=None):
    units, depth = saved_t.shape
    width = rows.shape[1]
    block = 1280 if width % 1280 == 0 else LANES

    def kernel(saved_ref, rows_ref, *refs):
        columns = pl.ds(pl.multiple_of(pl.program_id(0) * block, block), block)
        term = jnp.dot(saved_ref[...], rows_ref[:, columns], preferred_element_type=F32).astype(BF)
        if more is not None:
            term = (term.astype(F32) + refs[0][:, columns].astype(F32)).astype(BF)
        refs[-1][...] = term

    operands = [saved_t, rows] + ([] if more is None else [more])
    return pl.pallas_call(
        kernel,
        grid=(width // block,),
        in_specs=[pl.BlockSpec(memory_space=pltpu.VMEM)] * len(operands),
        out_specs=pl.BlockSpec((units, block), lambda j: (0, j)),
        out_shape=jax.ShapeDtypeStruct((units, width), BF)
        if more is None
        else pltpu.HBM((units, width), BF),
        compiler_params=pltpu.CompilerParams(vmem_limit_bytes=VMEM),
        cost_estimate=pl.CostEstimate(
            flops=2 * units * depth * width,
            bytes_accessed=2 * (units * depth + depth * width + units * width),
            transcendentals=0,
        ),
        name=name,
    )(*operands)


def _sum(parts):
    chips, units, width = parts.shape

    def kernel(parts_ref, out_ref):
        total = parts_ref[0].astype(F32)
        for i in range(1, chips):
            total += parts_ref[i].astype(F32)
        for i in range(units):
            out_ref[i, :, :] = total[i : i + 1, :]

    return pl.pallas_call(
        kernel,
        in_specs=[pl.BlockSpec(memory_space=pltpu.VMEM)],
        out_specs=pl.BlockSpec(memory_space=pltpu.VMEM),
        out_shape=jax.ShapeDtypeStruct((units, 1, width), F32),
        compiler_params=pltpu.CompilerParams(vmem_limit_bytes=VMEM),
        cost_estimate=pl.CostEstimate(
            flops=parts.size, bytes_accessed=2 * parts.size, transcendentals=0
        ),
        name="sum_parts",
    )(parts)


def body(grads, routes, gates, hidden, down_weight):
    groups = lax.axis_size("expert")
    replicas = lax.axis_size("replica")
    chips = replicas // 2
    width = grads.shape[2]
    units_dev = down_weight.shape[0]
    rows_dev = hidden.shape[1]
    units = hidden.shape[2]
    capacity = rows_dev // groups
    half = width // 2
    me = lax.axis_index("expert").astype(jnp.int32).reshape(1)
    core = lax.rem(lax.axis_index("replica"), 2)

    chip_groups = [[2 * q + c for q in range(chips)] for c in range(2)]

    def over_chips(array):
        return lax.all_to_all(
            array, "replica", split_axis=0, concat_axis=0, tiled=True, axis_index_groups=chip_groups
        )

    def other_core(array):
        return lax.ppermute(array, "replica", [(i, i ^ 1) for i in range(replicas)])

    weights_mine = over_chips(_copies(down_weight[:, 0, :], chips))

    own_first, own_second = _pack(grads[0], routes.transpose(2, 0, 1), gates[0].T)

    far = groups // 2
    relay = far - 3

    def shift(array, places):
        return lax.ppermute(array, "expert", [(i, (i + places) % groups) for i in range(groups)])

    got_first, got_second = {0: own_first}, {0: own_second}
    a_up = a_down = own_first
    b_up = b_down = own_second
    rows = None
    shape = (groups, capacity, width)

    def pick(rows, batch, name, after=()):
        firsts = [got_first[off] for off in batch]
        seconds = [got_second[off] for off in batch]
        return _select(me, batch, firsts, seconds, rows, shape, name, after)

    saved_mine, saved_other = _split(hidden[0], core.reshape(1), units_dev, own_first)
    for hop in range(1, relay + 1):
        if hop == 2:
            b_up, saved_mine, saved_other = lax.optimization_barrier(
                (b_up, saved_mine, saved_other)
            )
        if hop >= 3:
            a_up, rows = lax.optimization_barrier((a_up, rows))
        a_up, a_down = shift(a_up, 1), shift(a_down, -1)
        b_up, b_down = shift(b_up, 1), shift(b_down, -1)
        got_first[-hop], got_first[hop] = a_up, a_down
        got_second[-hop], got_second[hop] = b_up, b_down
        if hop == 2:
            rows = pick(rows, [0, -1, 1], "select_1", (weights_mine,))
        elif hop >= 3:
            rows = pick(rows, [1 - hop, hop - 1], f"select_{hop - 1}")

    far_down, rows = _forward(me, [(-3, (1,))], b_down, b_down, rows, "forward_far")
    far_down = shift(far_down, -3)
    up_2, up_3, up_1, rows = _forward(
        me, [(2, (0, 1)), (3, (0,)), (1, (0, 1))], a_up, b_up, rows, "forward_up"
    )
    down_2, down_1, rows = _forward(
        me, [(-2, (0, 1)), (-1, (0, 1))], a_down, b_down, rows, "forward_down"
    )
    rows = pick(rows, [-relay, relay], f"select_{relay}")
    up_2, down_2, far_up = shift(up_2, 2), shift(down_2, -2), shift(up_3, 3)
    up_1, down_1 = shift(up_1, 1), shift(down_1, -1)
    parts = [(-relay - 2, 0, up_2), (relay + 2, 0, down_2), (far, half, far_down)]
    rows = _place(me, parts, rows, "place_early")
    parts = [(-relay - 1, 0, up_1), (relay + 1, 0, down_1), (far, 0, far_up)]
    rows = _place(me, parts, rows, "place_late")
    rows = rows.reshape(rows_dev, width)

    other = _term(saved_other, rows, "term_other")
    arrived = other_core(other)
    pair = _term(saved_mine, rows, "term_pair", arrived)
    pair, rows = lax.optimization_barrier((pair, rows))
    sums = over_chips(pair.reshape(chips, units_dev, width))

    weights_other = other_core(weights_mine)
    both = jnp.where(
        core == 0,
        jnp.stack([weights_mine, weights_other], axis=1),
        jnp.stack([weights_other, weights_mine], axis=1),
    ).reshape(units, width)
    d_rows = lax.dot_general(rows, both, (((1,), (1,)), ((), ())), preferred_element_type=F32)
    d_hidden = d_rows.astype(BF)[None]
    sums, d_hidden = lax.optimization_barrier((sums, d_hidden))
    down_grad = _sum(sums)
    return (d_hidden, down_grad)


def solution(mesh):
    placed = (P("replica", "expert", None),) * 5
    return jax.shard_map(
        body,
        mesh=mesh,
        in_specs=placed,
        out_specs=(P("replica", "expert", None), P("replica", "expert", None)),
        check_vma=False,
    )
```

```python
import jax
import jax.numpy as jnp
from jax import lax
from jax.experimental import pallas as pl
from jax.experimental.pallas import tpu as pltpu
from jax.sharding import PartitionSpec as P

BF = jnp.bfloat16
F32 = jnp.float32
LANES = 128
INFO_ROWS = 8
VMEM = 16 << 20


def _pack_kernel(grads_ref, routes_ref, gates_ref, first_ref, second_ref):
    top, _, tokens = routes_ref.shape
    half = first_ref.shape[1]
    experts = 2 * INFO_ROWS
    first_ref[...] = grads_ref[:, 0:half]
    second_ref[0:tokens, :] = grads_ref[:, half:]
    gates = gates_ref[...].astype(F32)
    expert = lax.broadcasted_iota(jnp.int32, (experts, tokens), 0)
    gate = jnp.zeros((experts, tokens), F32)
    named = jnp.zeros((experts, tokens), F32)
    for k in range(top):
        hit = routes_ref[k] == expert
        gate = jnp.where(hit, gates[k : k + 1, :], gate)
        named = jnp.where(hit, 1.0, named)
    row = lax.broadcasted_iota(jnp.int32, (tokens, tokens), 0)
    col = lax.broadcasted_iota(jnp.int32, (tokens, tokens), 1)
    earlier = jnp.where(row < col, 1.0, 0.0).astype(BF)
    rank = jnp.dot(named.astype(BF), earlier, preferred_element_type=F32)
    slot = jnp.where(named > 0.5, rank, -1.0)
    n = INFO_ROWS
    parts = [slot[0:n], gate[0:n], slot[n : 2 * n], gate[n : 2 * n]]
    parts.append(jnp.zeros((n, half - 4 * tokens), F32))
    second_ref[tokens : tokens + n, :] = jnp.concatenate(parts, axis=1).astype(BF)


def _pack(grads, routes_t, gates_t):
    tokens, width = grads.shape
    half = width // 2
    return pl.pallas_call(
        _pack_kernel,
        out_shape=[
            jax.ShapeDtypeStruct((tokens, half), BF),
            jax.ShapeDtypeStruct((tokens + INFO_ROWS, half), BF),
        ],
        compiler_params=pltpu.CompilerParams(vmem_limit_bytes=VMEM),
        cost_estimate=pl.CostEstimate(
            flops=1 << 20, bytes_accessed=4 * tokens * width, transcendentals=0
        ),
        name="pack_tokens",
    )(grads, routes_t, gates_t)


def _split_kernel(units_dev, core_ref, hidden_ref, _, mine_ref, other_ref):
    units = hidden_ref.shape[1]
    half = units // 2
    row = lax.broadcasted_iota(jnp.int32, (half, units), 0)
    col = lax.broadcasted_iota(jnp.int32, (half, units), 1)
    even = row + units_dev * (row // units_dev)
    for flip, out_ref in ((0, mine_ref), (1, other_ref)):
        core = lax.rem(core_ref[0] + flip, 2)
        pick = jnp.where(col == even + core * units_dev, 1.0, 0.0).astype(BF)
        out_ref[...] = lax.dot_general(
            pick, hidden_ref[...], (((1,), (1,)), ((), ())), preferred_element_type=F32
        ).astype(BF)


def _split(hidden, core, units_dev, after):
    rows, units = hidden.shape

    def kernel(*refs):
        _split_kernel(units_dev, *refs)

    return pl.pallas_call(
        kernel,
        in_specs=[
            pl.BlockSpec(memory_space=pltpu.SMEM),
            pl.BlockSpec(memory_space=pltpu.VMEM),
            pl.BlockSpec(memory_space=pl.ANY),
        ],
        out_specs=[pl.BlockSpec(memory_space=pltpu.VMEM)] * 2,
        out_shape=[jax.ShapeDtypeStruct((units // 2, rows), BF)] * 2,
        compiler_params=pltpu.CompilerParams(vmem_limit_bytes=VMEM),
        cost_estimate=pl.CostEstimate(
            flops=2 * rows * units * units, bytes_accessed=4 * rows * units, transcendentals=0
        ),
        name="split_hidden",
    )(core, hidden, after)


def _picker(expert, second_ref, capacity):
    tokens = second_ref.shape[0] - INFO_ROWS
    info = second_ref[tokens : tokens + INFO_ROWS, 0 : 4 * tokens].astype(F32)
    info = jnp.where(expert >= INFO_ROWS, info[:, 2 * tokens :], info[:, : 2 * tokens])
    row = lax.broadcasted_iota(jnp.int32, info.shape, 0)
    mine = jnp.sum(jnp.where(row == lax.rem(expert, INFO_ROWS), info, 0.0), axis=0, keepdims=True)
    slot = lax.broadcasted_iota(jnp.int32, (capacity, tokens), 0).astype(F32)
    return jnp.where(mine[:, :tokens] == slot, mine[:, tokens:], 0.0).astype(BF)


def _select(me, offsets, firsts, seconds, rows, shape, name, after=()):
    count = len(offsets)
    groups, capacity, width = shape
    half = width // 2
    tokens = firsts[0].shape[0]

    def kernel(me_ref, *refs):
        out_ref = refs[-1]
        for i, off in enumerate(offsets):
            first_ref, second_ref = refs[i], refs[count + i]
            pick = _picker(me_ref[0], second_ref, capacity)
            place = lax.rem(me_ref[0] + (off + groups) % groups, groups)
            out_ref[place, :, :half] = jnp.dot(
                pick, first_ref[...], preferred_element_type=F32
            ).astype(BF)
            out_ref[place, :, half:] = jnp.dot(
                pick, second_ref[0:tokens, :], preferred_element_type=F32
            ).astype(BF)

    operands = list(firsts) + list(seconds) + ([] if rows is None else [rows])
    return pl.pallas_call(
        kernel,
        in_specs=[pl.BlockSpec(memory_space=pltpu.SMEM)]
        + [pl.BlockSpec(memory_space=pltpu.VMEM)] * len(operands)
        + [pl.BlockSpec(memory_space=pltpu.HBM)] * len(after),
        out_specs=pl.BlockSpec(memory_space=pltpu.VMEM),
        out_shape=jax.ShapeDtypeStruct(shape, BF),
        input_output_aliases={} if rows is None else {len(operands): 0},
        compiler_params=pltpu.CompilerParams(vmem_limit_bytes=VMEM),
        cost_estimate=pl.CostEstimate(
            flops=2 * count * capacity * tokens * width,
            bytes_accessed=2 * count * (tokens + capacity) * width,
            transcendentals=0,
        ),
        name=name,
    )(me, *operands, *after)


def _forward(me, sends, first, second, rows, name, after=()):
    tokens = second.shape[0] - INFO_ROWS
    half = first.shape[1]
    groups, capacity, _ = rows.shape
    widths = [half * len(chunks) for _, chunks in sends]

    def kernel(me_ref, first_ref, second_ref, _, *refs):
        for (step, chunks), out_ref in zip(sends, refs[len(after) :]):
            expert = lax.rem(me_ref[0] + (step + groups) % groups, groups)
            pick = _picker(expert, second_ref, capacity)
            for n, chunk in enumerate(chunks):
                block_ref = (first_ref, second_ref)[chunk]
                out_ref[:, n * half : (n + 1) * half] = jnp.dot(
                    pick, block_ref[0:tokens, :], preferred_element_type=F32
                ).astype(BF)

    return pl.pallas_call(
        kernel,
        in_specs=[pl.BlockSpec(memory_space=pltpu.SMEM)]
        + [pl.BlockSpec(memory_space=pltpu.VMEM)] * 3
        + [pl.BlockSpec(memory_space=pl.ANY)] * len(after),
        out_specs=[pl.BlockSpec(memory_space=pltpu.VMEM)] * (len(sends) + 1),
        out_shape=[jax.ShapeDtypeStruct((capacity, w), BF) for w in widths]
        + [jax.ShapeDtypeStruct(rows.shape, BF)],
        input_output_aliases={3: len(sends)},
        compiler_params=pltpu.CompilerParams(vmem_limit_bytes=VMEM),
        cost_estimate=pl.CostEstimate(
            flops=2 * capacity * tokens * sum(widths),
            bytes_accessed=2 * (tokens + capacity) * sum(widths),
            transcendentals=0,
        ),
        name=name,
    )(me, first, second, rows, *after)


def _place(me, parts, rows, name):
    groups, capacity, _ = rows.shape
    count = len(parts)

    def kernel(me_ref, *refs):
        out_ref = refs[-1]
        for (off, column, part), part_ref in zip(parts, refs):
            place = lax.rem(me_ref[0] + (off + groups) % groups, groups)
            out_ref[place, :, column : column + part.shape[1]] = part_ref[...]

    arrays = [part for _, _, part in parts]
    return pl.pallas_call(
        kernel,
        in_specs=[pl.BlockSpec(memory_space=pltpu.SMEM)]
        + [pl.BlockSpec(memory_space=pltpu.VMEM)] * (count + 1),
        out_specs=pl.BlockSpec(memory_space=pltpu.VMEM),
        out_shape=jax.ShapeDtypeStruct(rows.shape, BF),
        input_output_aliases={count + 1: 0},
        compiler_params=pltpu.CompilerParams(vmem_limit_bytes=VMEM),
        cost_estimate=pl.CostEstimate(
            flops=0, bytes_accessed=4 * sum(a.size for a in arrays), transcendentals=0
        ),
        name=name,
    )(me, *arrays, rows)


def _copies(array, copies):
    def kernel(array_ref, out_ref, sems):
        started = []
        for i in range(copies):
            started.append(pltpu.make_async_copy(array_ref, out_ref.at[i], sems.at[i]))
            started[-1].start()
        for copy in started:
            copy.wait()

    return pl.pallas_call(
        kernel,
        in_specs=[pl.BlockSpec(memory_space=pltpu.HBM)],
        out_specs=pl.BlockSpec(memory_space=pltpu.HBM),
        out_shape=pltpu.HBM((copies,) + array.shape, BF),
        scratch_shapes=[pltpu.SemaphoreType.DMA((copies,))],
        compiler_params=pltpu.CompilerParams(vmem_limit_bytes=VMEM),
        cost_estimate=pl.CostEstimate(
            flops=0, bytes_accessed=2 * (copies + 1) * array.size, transcendentals=0
        ),
        name="unit_copies",
    )(array)


def _term(saved_t, rows, name, more=None):
    units, depth = saved_t.shape
    width = rows.shape[1]
    block = 1280 if width % 1280 == 0 else LANES

    def kernel(saved_ref, rows_ref, *refs):
        columns = pl.ds(pl.multiple_of(pl.program_id(0) * block, block), block)
        term = jnp.dot(saved_ref[...], rows_ref[:, columns], preferred_element_type=F32).astype(BF)
        if more is not None:
            term = (term.astype(F32) + refs[0][:, columns].astype(F32)).astype(BF)
        refs[-1][...] = term

    operands = [saved_t, rows] + ([] if more is None else [more])
    return pl.pallas_call(
        kernel,
        grid=(width // block,),
        in_specs=[pl.BlockSpec(memory_space=pltpu.VMEM)] * len(operands),
        out_specs=pl.BlockSpec((units, block), lambda j: (0, j)),
        out_shape=jax.ShapeDtypeStruct((units, width), BF)
        if more is None
        else pltpu.HBM((units, width), BF),
        compiler_params=pltpu.CompilerParams(vmem_limit_bytes=VMEM),
        cost_estimate=pl.CostEstimate(
            flops=2 * units * depth * width,
            bytes_accessed=2 * (units * depth + depth * width + units * width),
            transcendentals=0,
        ),
        name=name,
    )(*operands)


def _sum(parts):
    chips, units, width = parts.shape

    def kernel(parts_ref, out_ref):
        total = parts_ref[0].astype(F32)
        for i in range(1, chips):
            total += parts_ref[i].astype(F32)
        for i in range(units):
            out_ref[i, :, :] = total[i : i + 1, :]

    return pl.pallas_call(
        kernel,
        in_specs=[pl.BlockSpec(memory_space=pltpu.VMEM)],
        out_specs=pl.BlockSpec(memory_space=pltpu.VMEM),
        out_shape=jax.ShapeDtypeStruct((units, 1, width), F32),
        compiler_params=pltpu.CompilerParams(vmem_limit_bytes=VMEM),
        cost_estimate=pl.CostEstimate(
            flops=parts.size, bytes_accessed=2 * parts.size, transcendentals=0
        ),
        name="sum_parts",
    )(parts)


def body(grads, routes, gates, hidden, down_weight):
    groups = lax.axis_size("expert")
    replicas = lax.axis_size("replica")
    chips = replicas // 2
    width = grads.shape[2]
    units_dev = down_weight.shape[0]
    rows_dev = hidden.shape[1]
    units = hidden.shape[2]
    capacity = rows_dev // groups
    half = width // 2
    me = lax.axis_index("expert").astype(jnp.int32).reshape(1)
    core = lax.rem(lax.axis_index("replica"), 2)

    chip_groups = [[2 * q + c for q in range(chips)] for c in range(2)]

    def over_chips(array):
        return lax.all_to_all(
            array, "replica", split_axis=0, concat_axis=0, tiled=True, axis_index_groups=chip_groups
        )

    def other_core(array):
        return lax.ppermute(array, "replica", [(i, i ^ 1) for i in range(replicas)])

    weights_mine = over_chips(_copies(down_weight[:, 0, :], chips))

    own_first, own_second = _pack(grads[0], routes.transpose(2, 0, 1), gates[0].T)

    far = groups // 2
    relay = far - 3

    def shift(array, places):
        return lax.ppermute(array, "expert", [(i, (i + places) % groups) for i in range(groups)])

    got_first, got_second = {0: own_first}, {0: own_second}
    a_up = a_down = own_first
    b_up = b_down = own_second
    rows = None
    shape = (groups, capacity, width)

    def pick(rows, batch, name, after=()):
        firsts = [got_first[off] for off in batch]
        seconds = [got_second[off] for off in batch]
        return _select(me, batch, firsts, seconds, rows, shape, name, after)

    saved_mine, saved_other = _split(hidden[0], core.reshape(1), units_dev, own_first)
    for hop in range(1, relay + 1):
        if hop == 2:
            b_up, b_down, saved_mine, saved_other = lax.optimization_barrier(
                (b_up, b_down, saved_mine, saved_other)
            )
        if hop >= 3:
            a_up, rows = lax.optimization_barrier((a_up, rows))
        a_up, a_down = shift(a_up, 1), shift(a_down, -1)
        b_up, b_down = shift(b_up, 1), shift(b_down, -1)
        got_first[-hop], got_first[hop] = a_up, a_down
        got_second[-hop], got_second[hop] = b_up, b_down
        if hop == 2:
            rows = pick(rows, [0, -1, 1], "select_1", (weights_mine,))
        elif hop >= 3:
            rows = pick(rows, [1 - hop, hop - 1], f"select_{hop - 1}")

    far_down, rows = _forward(me, [(-3, (1,))], b_down, b_down, rows, "forward_far")
    far_down = shift(far_down, -3)
    up_2, up_3, up_1, rows = _forward(
        me, [(2, (0, 1)), (3, (0,)), (1, (0, 1))], a_up, b_up, rows, "forward_up"
    )
    down_2, down_1, rows = _forward(
        me, [(-2, (0, 1)), (-1, (0, 1))], a_down, b_down, rows, "forward_down"
    )
    rows = pick(rows, [-relay, relay], f"select_{relay}")
    up_2, down_2, far_up = shift(up_2, 2), shift(down_2, -2), shift(up_3, 3)
    up_1, down_1 = shift(up_1, 1), shift(down_1, -1)
    parts = [(-relay - 2, 0, up_2), (relay + 2, 0, down_2), (far, half, far_down)]
    rows = _place(me, parts, rows, "place_early")
    parts = [(-relay - 1, 0, up_1), (relay + 1, 0, down_1), (far, 0, far_up)]
    rows = _place(me, parts, rows, "place_late")
    rows = rows.reshape(rows_dev, width)

    other = _term(saved_other, rows, "term_other")
    arrived = other_core(other)
    pair = _term(saved_mine, rows, "term_pair", arrived)
    pair, rows = lax.optimization_barrier((pair, rows))
    sums = over_chips(pair.reshape(chips, units_dev, width))

    weights_other = other_core(weights_mine)
    both = jnp.where(
        core == 0,
        jnp.stack([weights_mine, weights_other], axis=1),
        jnp.stack([weights_other, weights_mine], axis=1),
    ).reshape(units, width)
    d_rows = lax.dot_general(rows, both, (((1,), (1,)), ((), ())), preferred_element_type=F32)
    d_hidden = d_rows.astype(BF)[None]
    sums, d_hidden = lax.optimization_barrier((sums, d_hidden))
    down_grad = _sum(sums)
    return (d_hidden, down_grad)


def solution(mesh):
    placed = (P("replica", "expert", None),) * 5
    return jax.shard_map(
        body,
        mesh=mesh,
        in_specs=placed,
        out_specs=(P("replica", "expert", None), P("replica", "expert", None)),
        check_vma=False,
    )
```

```python
import jax
import jax.numpy as jnp
from jax import lax
from jax.experimental import pallas as pl
from jax.experimental.pallas import tpu as pltpu
from jax.sharding import PartitionSpec as P

BF = jnp.bfloat16
F32 = jnp.float32
LANES = 128
INFO_ROWS = 8
VMEM = 16 << 20


def _pack_kernel(grads_ref, routes_ref, gates_ref, first_ref, second_ref):
    top, _, tokens = routes_ref.shape
    half = first_ref.shape[1]
    experts = 2 * INFO_ROWS
    first_ref[...] = grads_ref[:, 0:half]
    second_ref[0:tokens, :] = grads_ref[:, half:]
    gates = gates_ref[...].astype(F32)
    expert = lax.broadcasted_iota(jnp.int32, (experts, tokens), 0)
    gate = jnp.zeros((experts, tokens), F32)
    named = jnp.zeros((experts, tokens), F32)
    for k in range(top):
        hit = routes_ref[k] == expert
        gate = jnp.where(hit, gates[k : k + 1, :], gate)
        named = jnp.where(hit, 1.0, named)
    row = lax.broadcasted_iota(jnp.int32, (tokens, tokens), 0)
    col = lax.broadcasted_iota(jnp.int32, (tokens, tokens), 1)
    earlier = jnp.where(row < col, 1.0, 0.0).astype(BF)
    rank = jnp.dot(named.astype(BF), earlier, preferred_element_type=F32)
    slot = jnp.where(named > 0.5, rank, -1.0)
    n = INFO_ROWS
    parts = [slot[0:n], gate[0:n], slot[n : 2 * n], gate[n : 2 * n]]
    parts.append(jnp.zeros((n, half - 4 * tokens), F32))
    second_ref[tokens : tokens + n, :] = jnp.concatenate(parts, axis=1).astype(BF)


def _pack(grads, routes_t, gates_t):
    tokens, width = grads.shape
    half = width // 2
    return pl.pallas_call(
        _pack_kernel,
        out_shape=[
            jax.ShapeDtypeStruct((tokens, half), BF),
            jax.ShapeDtypeStruct((tokens + INFO_ROWS, half), BF),
        ],
        compiler_params=pltpu.CompilerParams(vmem_limit_bytes=VMEM),
        cost_estimate=pl.CostEstimate(
            flops=1 << 20, bytes_accessed=4 * tokens * width, transcendentals=0
        ),
        name="pack_tokens",
    )(grads, routes_t, gates_t)


def _split_kernel(units_dev, core_ref, hidden_ref, _, mine_ref, other_ref):
    units = hidden_ref.shape[1]
    half = units // 2
    row = lax.broadcasted_iota(jnp.int32, (half, units), 0)
    col = lax.broadcasted_iota(jnp.int32, (half, units), 1)
    even = row + units_dev * (row // units_dev)
    for flip, out_ref in ((0, mine_ref), (1, other_ref)):
        core = lax.rem(core_ref[0] + flip, 2)
        pick = jnp.where(col == even + core * units_dev, 1.0, 0.0).astype(BF)
        out_ref[...] = lax.dot_general(
            pick, hidden_ref[...], (((1,), (1,)), ((), ())), preferred_element_type=F32
        ).astype(BF)


def _split(hidden, core, units_dev, after):
    rows, units = hidden.shape

    def kernel(*refs):
        _split_kernel(units_dev, *refs)

    return pl.pallas_call(
        kernel,
        in_specs=[
            pl.BlockSpec(memory_space=pltpu.SMEM),
            pl.BlockSpec(memory_space=pltpu.VMEM),
            pl.BlockSpec(memory_space=pl.ANY),
        ],
        out_specs=[pl.BlockSpec(memory_space=pltpu.VMEM)] * 2,
        out_shape=[jax.ShapeDtypeStruct((units // 2, rows), BF)] * 2,
        compiler_params=pltpu.CompilerParams(vmem_limit_bytes=VMEM),
        cost_estimate=pl.CostEstimate(
            flops=2 * rows * units * units, bytes_accessed=4 * rows * units, transcendentals=0
        ),
        name="split_hidden",
    )(core, hidden, after)


def _picker(expert, second_ref, capacity):
    tokens = second_ref.shape[0] - INFO_ROWS
    info = second_ref[tokens : tokens + INFO_ROWS, 0 : 4 * tokens].astype(F32)
    info = jnp.where(expert >= INFO_ROWS, info[:, 2 * tokens :], info[:, : 2 * tokens])
    row = lax.broadcasted_iota(jnp.int32, info.shape, 0)
    mine = jnp.sum(jnp.where(row == lax.rem(expert, INFO_ROWS), info, 0.0), axis=0, keepdims=True)
    slot = lax.broadcasted_iota(jnp.int32, (capacity, tokens), 0).astype(F32)
    return jnp.where(mine[:, :tokens] == slot, mine[:, tokens:], 0.0).astype(BF)


def _select(me, offsets, firsts, seconds, rows, shape, name, after=()):
    count = len(offsets)
    groups, capacity, width = shape
    half = width // 2
    tokens = firsts[0].shape[0]

    def kernel(me_ref, *refs):
        out_ref = refs[-1]
        for i, off in enumerate(offsets):
            first_ref, second_ref = refs[i], refs[count + i]
            pick = _picker(me_ref[0], second_ref, capacity)
            place = lax.rem(me_ref[0] + (off + groups) % groups, groups)
            out_ref[place, :, :half] = jnp.dot(
                pick, first_ref[...], preferred_element_type=F32
            ).astype(BF)
            out_ref[place, :, half:] = jnp.dot(
                pick, second_ref[0:tokens, :], preferred_element_type=F32
            ).astype(BF)

    operands = list(firsts) + list(seconds) + ([] if rows is None else [rows])
    return pl.pallas_call(
        kernel,
        in_specs=[pl.BlockSpec(memory_space=pltpu.SMEM)]
        + [pl.BlockSpec(memory_space=pltpu.VMEM)] * len(operands)
        + [pl.BlockSpec(memory_space=pltpu.HBM)] * len(after),
        out_specs=pl.BlockSpec(memory_space=pltpu.VMEM),
        out_shape=jax.ShapeDtypeStruct(shape, BF),
        input_output_aliases={} if rows is None else {len(operands): 0},
        compiler_params=pltpu.CompilerParams(vmem_limit_bytes=VMEM),
        cost_estimate=pl.CostEstimate(
            flops=2 * count * capacity * tokens * width,
            bytes_accessed=2 * count * (tokens + capacity) * width,
            transcendentals=0,
        ),
        name=name,
    )(me, *operands, *after)


def _forward(me, sends, first, second, rows, name, after=()):
    tokens = second.shape[0] - INFO_ROWS
    half = first.shape[1]
    groups, capacity, _ = rows.shape
    widths = [half * len(chunks) for _, chunks in sends]

    def kernel(me_ref, first_ref, second_ref, _, *refs):
        for (step, chunks), out_ref in zip(sends, refs[len(after) :]):
            expert = lax.rem(me_ref[0] + (step + groups) % groups, groups)
            pick = _picker(expert, second_ref, capacity)
            for n, chunk in enumerate(chunks):
                block_ref = (first_ref, second_ref)[chunk]
                out_ref[:, n * half : (n + 1) * half] = jnp.dot(
                    pick, block_ref[0:tokens, :], preferred_element_type=F32
                ).astype(BF)

    return pl.pallas_call(
        kernel,
        in_specs=[pl.BlockSpec(memory_space=pltpu.SMEM)]
        + [pl.BlockSpec(memory_space=pltpu.VMEM)] * 3
        + [pl.BlockSpec(memory_space=pl.ANY)] * len(after),
        out_specs=[pl.BlockSpec(memory_space=pltpu.VMEM)] * (len(sends) + 1),
        out_shape=[jax.ShapeDtypeStruct((capacity, w), BF) for w in widths]
        + [jax.ShapeDtypeStruct(rows.shape, BF)],
        input_output_aliases={3: len(sends)},
        compiler_params=pltpu.CompilerParams(vmem_limit_bytes=VMEM),
        cost_estimate=pl.CostEstimate(
            flops=2 * capacity * tokens * sum(widths),
            bytes_accessed=2 * (tokens + capacity) * sum(widths),
            transcendentals=0,
        ),
        name=name,
    )(me, first, second, rows, *after)


def _place(me, parts, rows, name):
    groups, capacity, _ = rows.shape
    count = len(parts)

    def kernel(me_ref, *refs):
        out_ref = refs[-1]
        for (off, column, part), part_ref in zip(parts, refs):
            place = lax.rem(me_ref[0] + (off + groups) % groups, groups)
            out_ref[place, :, column : column + part.shape[1]] = part_ref[...]

    arrays = [part for _, _, part in parts]
    return pl.pallas_call(
        kernel,
        in_specs=[pl.BlockSpec(memory_space=pltpu.SMEM)]
        + [pl.BlockSpec(memory_space=pltpu.VMEM)] * (count + 1),
        out_specs=pl.BlockSpec(memory_space=pltpu.VMEM),
        out_shape=jax.ShapeDtypeStruct(rows.shape, BF),
        input_output_aliases={count + 1: 0},
        compiler_params=pltpu.CompilerParams(vmem_limit_bytes=VMEM),
        cost_estimate=pl.CostEstimate(
            flops=0, bytes_accessed=4 * sum(a.size for a in arrays), transcendentals=0
        ),
        name=name,
    )(me, *arrays, rows)


def _term(saved_t, rows, name, more=None):
    units, depth = saved_t.shape
    width = rows.shape[1]
    block = 1280 if width % 1280 == 0 else LANES

    def kernel(saved_ref, rows_ref, *refs):
        columns = pl.ds(pl.multiple_of(pl.program_id(0) * block, block), block)
        term = jnp.dot(saved_ref[...], rows_ref[:, columns], preferred_element_type=F32).astype(BF)
        if more is not None:
            term = (term.astype(F32) + refs[0][:, columns].astype(F32)).astype(BF)
        refs[-1][...] = term

    operands = [saved_t, rows] + ([] if more is None else [more])
    return pl.pallas_call(
        kernel,
        grid=(width // block,),
        in_specs=[pl.BlockSpec(memory_space=pltpu.VMEM)] * len(operands),
        out_specs=pl.BlockSpec((units, block), lambda j: (0, j)),
        out_shape=jax.ShapeDtypeStruct((units, width), BF)
        if more is None
        else pltpu.HBM((units, width), BF),
        compiler_params=pltpu.CompilerParams(vmem_limit_bytes=VMEM),
        cost_estimate=pl.CostEstimate(
            flops=2 * units * depth * width,
            bytes_accessed=2 * (units * depth + depth * width + units * width),
            transcendentals=0,
        ),
        name=name,
    )(*operands)


def _sum(parts):
    chips, units, width = parts.shape

    def kernel(parts_ref, out_ref):
        total = parts_ref[0].astype(F32)
        for i in range(1, chips):
            total += parts_ref[i].astype(F32)
        for i in range(units):
            out_ref[i, :, :] = total[i : i + 1, :]

    return pl.pallas_call(
        kernel,
        in_specs=[pl.BlockSpec(memory_space=pltpu.VMEM)],
        out_specs=pl.BlockSpec(memory_space=pltpu.VMEM),
        out_shape=jax.ShapeDtypeStruct((units, 1, width), F32),
        compiler_params=pltpu.CompilerParams(vmem_limit_bytes=VMEM),
        cost_estimate=pl.CostEstimate(
            flops=parts.size, bytes_accessed=2 * parts.size, transcendentals=0
        ),
        name="sum_parts",
    )(parts)


def body(grads, routes, gates, hidden, down_weight):
    groups = lax.axis_size("expert")
    replicas = lax.axis_size("replica")
    chips = replicas // 2
    width = grads.shape[2]
    units_dev = down_weight.shape[0]
    rows_dev = hidden.shape[1]
    units = hidden.shape[2]
    capacity = rows_dev // groups
    half = width // 2
    me = lax.axis_index("expert").astype(jnp.int32).reshape(1)
    core = lax.rem(lax.axis_index("replica"), 2)

    chip_groups = [[2 * q + c for q in range(chips)] for c in range(2)]

    def over_chips(array):
        return lax.all_to_all(
            array, "replica", split_axis=0, concat_axis=0, tiled=True, axis_index_groups=chip_groups
        )

    def other_core(array):
        return lax.ppermute(array, "replica", [(i, i ^ 1) for i in range(replicas)])

    weights_mine = over_chips(
        jnp.broadcast_to(down_weight[:, 0, :][None], (chips, units_dev, width))
    )

    own_first, own_second = _pack(grads[0], routes.transpose(2, 0, 1), gates[0].T)

    far = groups // 2
    relay = far - 3

    def shift(array, places):
        return lax.ppermute(array, "expert", [(i, (i + places) % groups) for i in range(groups)])

    got_first, got_second = {0: own_first}, {0: own_second}
    a_up = a_down = own_first
    b_up = b_down = own_second
    rows = None
    shape = (groups, capacity, width)

    def pick(rows, batch, name, after=()):
        firsts = [got_first[off] for off in batch]
        seconds = [got_second[off] for off in batch]
        return _select(me, batch, firsts, seconds, rows, shape, name, after)

    saved_mine, saved_other = _split(hidden[0], core.reshape(1), units_dev, own_first)
    for hop in range(1, relay + 1):
        if hop == 2:
            b_up, b_down, saved_mine, saved_other = lax.optimization_barrier(
                (b_up, b_down, saved_mine, saved_other)
            )
        if hop >= 3:
            a_up, rows = lax.optimization_barrier((a_up, rows))
        a_up, a_down = shift(a_up, 1), shift(a_down, -1)
        b_up, b_down = shift(b_up, 1), shift(b_down, -1)
        got_first[-hop], got_first[hop] = a_up, a_down
        got_second[-hop], got_second[hop] = b_up, b_down
        if hop == 2:
            rows = pick(rows, [0, -1, 1], "select_1", (weights_mine,))
        elif hop >= 3:
            rows = pick(rows, [1 - hop, hop - 1], f"select_{hop - 1}")

    far_down, rows = _forward(me, [(-3, (1,))], b_down, b_down, rows, "forward_far")
    far_down = shift(far_down, -3)
    up_2, up_3, up_1, rows = _forward(
        me, [(2, (0, 1)), (3, (0,)), (1, (0, 1))], a_up, b_up, rows, "forward_up"
    )
    down_2, down_1, rows = _forward(
        me, [(-2, (0, 1)), (-1, (0, 1))], a_down, b_down, rows, "forward_down"
    )
    rows = pick(rows, [-relay, relay], f"select_{relay}")
    up_2, down_2, far_up = shift(up_2, 2), shift(down_2, -2), shift(up_3, 3)
    up_1, down_1 = shift(up_1, 1), shift(down_1, -1)
    parts = [(-relay - 2, 0, up_2), (relay + 2, 0, down_2), (far, half, far_down)]
    rows = _place(me, parts, rows, "place_early")
    parts = [(-relay - 1, 0, up_1), (relay + 1, 0, down_1), (far, 0, far_up)]
    rows = _place(me, parts, rows, "place_late")
    rows = rows.reshape(rows_dev, width)

    other = _term(saved_other, rows, "term_other")
    arrived = other_core(other)
    pair = _term(saved_mine, rows, "term_pair", arrived)
    pair, rows = lax.optimization_barrier((pair, rows))
    sums = over_chips(pair.reshape(chips, units_dev, width))

    weights_other = other_core(weights_mine)
    both = jnp.where(
        core == 0,
        jnp.stack([weights_mine, weights_other], axis=1),
        jnp.stack([weights_other, weights_mine], axis=1),
    ).reshape(units, width)
    d_rows = lax.dot_general(rows, both, (((1,), (1,)), ((), ())), preferred_element_type=F32)
    d_hidden = d_rows.astype(BF)[None]
    sums, d_hidden = lax.optimization_barrier((sums, d_hidden))
    down_grad = _sum(sums)
    return (d_hidden, down_grad)


def solution(mesh):
    placed = (P("replica", "expert", None),) * 5
    return jax.shard_map(
        body,
        mesh=mesh,
        in_specs=placed,
        out_specs=(P("replica", "expert", None), P("replica", "expert", None)),
        check_vma=False,
    )
```
